512 devices in a mesh: node: 32 (over x, y_lo, core), local: 16 (over z, y_hi).
Axes of the slice: x: 4, y: 8 (y_hi: 2, y_lo: 4; y = y_hi * 4 + y_lo), z: 8, core: 2. Of those that a mesh axis runs over, the one named last changes fastest.
Arguments:
- hidden: bfloat16 [65536, 5120], P(('node', 'local')), may hold values from -6 to 6
- gain: float32 [5120], replicated, may hold values from 0.1 to 1.9
- cotangent: bfloat16 [65536, 128], P(('node', 'local')), may hold values from -6 to 6
- weight: bfloat16 [5120, 128], P('local'), may hold values from -0.078125 to 0.078125
- momentum: float32 [32, 5120, 128], P('node', 'local'), may hold values from -1536 to 1536
- indices: int32 [160, 32], P('local'), may hold values from 0 to 4095, as said below
Outputs:
- new_weight: bfloat16 [5120, 128], replicated
- new_momentum: float32 [32, 5120, 128], P('node', 'local')
- input_grad: bfloat16 [65536, 5120], P(('node', 'local'))
The draws below stay inside these ranges and needn't reach their ends.
Inputs may be any that keep to these rules, and one draw needn't show every extreme that they name: `indices`: each row lists 32 different positions in a block, as row * 64 + column.
All inputs are finite; a program needn't handle non-finite values.
Results may differ from the reference program's by a relative error of at most 0.0006.
Values may be sent and summed in bfloat16 or wider, within the bound.
No kernel may reach another device: no remote copies, remote signals or barrier semaphores. Data moves between devices by JAX's collectives and lax.ppermute only.
A program may use at most 64 MiB of HBM per device.

```python
import jax
import jax.numpy as jnp
from jax import lax

D = 5120
HD = 128
TOK_DEV = 128
BLOCK = 64
TOPK = 32
TOKENS = 65536
GROUPS = 160
N_NODE = 32
N_LOCAL = 16


def draw_indices(key, part):
    key = jax.random.fold_in(key, 7)
    span = BLOCK * BLOCK
    base = jnp.tile(jnp.arange(span, dtype=jnp.int32)[None, :], (GROUPS, 1))
    mixed = jax.random.permutation(key, base, axis=1, independent=True)
    chosen = mixed[:, :TOPK]
    inner = jax.random.permutation(jax.random.fold_in(key, 1), jnp.arange(1, span - 1, dtype=jnp.int32))[:TOPK - 2]
    first = jnp.concatenate([jnp.array([0, span - 1], dtype=jnp.int32), inner])
    return chosen.at[0].set(first)


def block_levels(key, dims, shards, smallest, largest):
    loudness = 1.0
    for position, blocks in shards:
        draws = jax.random.uniform(jax.random.fold_in(jax.random.fold_in(key, 6), position), (blocks,), jnp.float32, smallest / len(shards), largest / len(shards))
        loudness = loudness * jnp.repeat(jnp.exp(draws), dims[position] // blocks).reshape((-1,) + (1,) * (len(dims) - 1 - position))
    return loudness


def normal_values(own_key, dims, width, limit, cuts=(), kind=jnp.bfloat16):
    drawn = jax.random.normal(own_key, dims, jnp.float32) * width
    if len(cuts) > 0:
        drawn = block_levels(own_key, dims, cuts, -0.22, 0.18) * drawn
    return jnp.clip(drawn, min=-limit, max=limit).astype(kind)


def setup_inputs(seed: int = 0) -> dict:
    keys = jax.random.split(jax.random.key(seed), 7)
    hidden = normal_values(keys[0], (TOKENS, D), 1.0, 6.0, ((0, 512),))
    gain = jnp.clip(1.0 + 0.18 * jax.random.normal(keys[1], (D,), jnp.float32), 0.1, 1.9)
    cotangent = normal_values(keys[2], (TOKENS, HD), 1.0, 6.0, ((0, 512),))
    weight = normal_values(keys[3], (D, HD), D ** -0.5, 0.078125, ((0, 16),))
    momentum = normal_values(keys[4], (N_NODE, D, HD), 256.0, 1536.0, ((0, 32), (1, 16)), jnp.float32)
    indices = draw_indices(jax.random.fold_in(keys[6], 71), 0)
    return dict(hidden=hidden, gain=gain, cotangent=cotangent, weight=weight, momentum=momentum, indices=indices)


epsilon = 1e-06
decay_rate = 0.9
learn_rate = 0.01

def dct_table():
    freq = jnp.arange(BLOCK, dtype=jnp.float32)[:, None]
    place = jnp.arange(BLOCK, dtype=jnp.float32)[None, :]
    wave = jnp.cos(jnp.pi * (2.0 * place + 1.0) * freq / (2.0 * BLOCK))
    norm_row = jnp.where(freq == 0.0, jnp.sqrt(1.0 / BLOCK), jnp.sqrt(2.0 / BLOCK))
    return wave * norm_row

def forward(field, table):
    blocks = field.reshape(field.shape[0] // BLOCK, BLOCK, field.shape[1] // BLOCK, BLOCK)
    spec = jnp.einsum('kn,rncm,lm->rckl', table, blocks, table, precision=lax.Precision.HIGHEST)
    return spec.reshape(-1, BLOCK * BLOCK)

def inverse(flat, height, breadth, table):
    spec = flat.reshape(height // BLOCK, breadth // BLOCK, BLOCK, BLOCK)
    field = jnp.einsum('kn,rckl,lm->rncm', table, spec, table, precision=lax.Precision.HIGHEST)
    return field.reshape(height, breadth)

def spread(values, indices):
    empty = jnp.zeros((indices.shape[0], BLOCK * BLOCK), values.dtype)
    rows_at = jnp.arange(indices.shape[0], dtype=jnp.int32)[:, None]
    return empty.at[rows_at, indices].set(values)

def reference(hidden, gain, cotangent, weight, momentum, indices):
    table = dct_table()
    node_hidden = hidden.reshape(N_NODE, N_LOCAL * TOK_DEV, D)
    node_cot = cotangent.reshape(N_NODE, N_LOCAL * TOK_DEV, HD)
    gain_wide = gain.astype(jnp.float32)

    def one_node(pair):
        rows_h, rows_c = pair
        wide = rows_h.astype(jnp.float32)
        scale = lax.rsqrt(lax.optimization_barrier(jnp.mean(wide * wide, axis=1, keepdims=True)) + epsilon)
        normed = (wide * scale * gain_wide).astype(jnp.bfloat16)
        grad = lax.dot_general(normed, rows_c, (((0,), (0,)), ((), ())), preferred_element_type=jnp.float32)
        dnormed = lax.dot_general(rows_c, weight, (((1,), (1,)), ((), ())), preferred_element_type=jnp.float32)
        gained = gain_wide * dnormed
        back = scale * gained - wide * scale ** 3 * lax.optimization_barrier(jnp.mean(wide * gained, axis=1, keepdims=True))
        return (grad, back.astype(jnp.bfloat16))
    grads, backs = lax.map(one_node, (node_hidden, node_cot))
    middle = decay_rate * momentum + grads
    spectra = jax.vmap(lambda f: forward(f, table))(middle)
    wide_idx = jnp.broadcast_to(indices[None], (N_NODE,) + indices.shape)
    picked = jnp.take_along_axis(spectra, wide_idx, axis=2)
    sent = jax.vmap(lambda p: inverse(spread(p, indices), D, HD, table))(picked)
    new_momentum = middle - sent
    total = lax.optimization_barrier(jnp.sum(picked, axis=0)) / N_NODE
    field = inverse(spread(total, indices), D, HD, table)
    new_weight = (weight.astype(jnp.float32) - learn_rate * jnp.tanh(field)).astype(jnp.bfloat16)
    return (new_weight, new_momentum, backs.reshape(TOKENS, D))
```

```python
import functools

import jax
import jax.numpy as jnp
from jax import lax
from jax.experimental import pallas as pl
from jax.experimental.pallas import tpu as pltpu
from jax.sharding import PartitionSpec as P

epsilon = 1e-06
decay_rate = 0.9
learn_rate = 0.01
side = 64
pair = 128
f32 = jnp.float32
bf16 = jnp.bfloat16

z_groups = [[2 * z + h for z in range(8)] for h in range(2)]
x_groups = [[8 * x + r for x in range(4)] for r in range(8)]
core_groups = [[2 * i, 2 * i + 1] for i in range(16)]


def whole_mesh(move):
    def index(x, y, z, core):
        return ((x * 4 + y % 4) * 2 + core) * 16 + z * 2 + y // 4

    places = [(x, y, z, c) for x in range(4) for y in range(8) for z in range(8) for c in range(2)]
    return [(index(*place), index(*move(*place))) for place in places]


def hop(value, move):
    return lax.ppermute(value, ("node", "local"), whole_mesh(move))


def dct_table():
    freq = jnp.arange(side, dtype=f32)[:, None]
    place = jnp.arange(side, dtype=f32)[None, :]
    wave = jnp.cos(jnp.pi * (2.0 * place + 1.0) * freq / (2.0 * side))
    norm_row = jnp.where(freq == 0.0, jnp.sqrt(1.0 / side), jnp.sqrt(2.0 / side))
    return wave * norm_row


def split2(value):
    high = value.astype(bf16)
    return high, (value - high.astype(f32)).astype(bf16)


def pair_table():
    turned = dct_table().T
    empty = jnp.zeros_like(turned)
    wide = jnp.block([[turned, empty], [empty, turned]])
    high = lax.reduce_precision(wide, exponent_bits=8, mantissa_bits=7)
    return jnp.concatenate([high, wide - high], axis=0).astype(bf16)


def dot(a, b, dims):
    return lax.dot_general(a, b, (dims, ((), ())), preferred_element_type=f32)


def waves(table, spots):
    at = lax.broadcasted_iota(jnp.int32, (pair, pair), 0)
    chosen = jnp.where(at == spots, 1.0, 0.0).astype(bf16)
    both = dot(table, chosen, ((1,), (0,)))
    return both[:pair].astype(bf16), both[pair:].astype(bf16)


def front_kernel(hidden_ref, gain_ref, cot_ref, message_ref, high_ref, low_ref):
    wide = hidden_ref[...].astype(f32)
    features = wide.shape[1]
    owners, tall, _ = message_ref.shape
    rows = features // owners
    scale = lax.rsqrt(jnp.sum(wide * wide, axis=1, keepdims=True) * (1.0 / features) + epsilon)
    cot = cot_ref[...]
    for piece in range(owners // 2):
        at = slice(piece * 2 * rows, (piece + 1) * 2 * rows)
        normed = (hidden_ref[:, at].astype(f32) * scale * gain_ref[:, at]).astype(bf16)
        turned = dot(cot, normed, ((0,), (0,)))
        high, low = split2(turned)
        high_ref[:, at] = high
        low_ref[:, at] = low
        term = dot(normed, cot, ((0,), (0,)))
        for half in range(2):
            own = term[half * rows : (half + 1) * rows]
            top = jnp.max(jnp.abs(own), axis=0, keepdims=True)
            power = jnp.ceil(jnp.log2(top * (1.0 / 32000.0)))
            power = jnp.clip(power, -120.0, 120.0)
            whole = jnp.round(own * jnp.exp2(-power)).astype(jnp.int32)
            message_ref[2 * piece + half, 0:rows, :] = whole.astype(jnp.int16)
            message_ref[2 * piece + half, rows:tall, :] = jnp.broadcast_to(
                power.astype(jnp.int32), (tall - rows, pair)
            ).astype(jnp.int16)


def front(hidden, gain, cot, owners):
    tokens, features = hidden.shape
    rows = features // owners
    return pl.pallas_call(
        front_kernel,
        out_shape=(
            jax.ShapeDtypeStruct((owners, rows + 16, pair), jnp.int16),
            jax.ShapeDtypeStruct((pair, features), bf16),
            jax.ShapeDtypeStruct((pair, features), bf16),
        ),
        compiler_params=pltpu.CompilerParams(vmem_limit_bytes=40 * 2**20),
        name="front",
    )(hidden, gain, cot)


def own_kernel(table_ref, row_ref, col_ref, momentum_ref, row_waves_ref, col_waves_ref, picked_ref):
    for q in range(row_ref.shape[0]):
        row_high, row_low = waves(table_ref[...], row_ref[q : q + 1, :])
        col_high, col_low = waves(table_ref[...], col_ref[q : q + 1, :])
        row_waves = row_high.astype(f32) + row_low.astype(f32)
        col_waves = col_high.astype(f32) + col_low.astype(f32)
        row_waves_ref[q] = row_waves
        col_waves_ref[q] = col_waves
        tile = decay_rate * momentum_ref[q * pair : (q + 1) * pair, :]
        half = lax.dot_general(
            tile, row_waves, (((0,), (0,)), ((), ())), precision=lax.Precision.HIGHEST, preferred_element_type=f32
        )
        picked_ref[q : q + 1, :] = jnp.sum(half * col_waves, axis=0, keepdims=True)


def own_waves(table, rows, cols, momentum):
    tiles = rows.shape[0]
    return pl.pallas_call(
        own_kernel,
        out_shape=(
            jax.ShapeDtypeStruct((tiles, pair, pair), f32),
            jax.ShapeDtypeStruct((tiles, pair, pair), f32),
            jax.ShapeDtypeStruct((tiles, pair), f32),
        ),
        name="own_waves",
    )(table, rows, cols, momentum)


def pick_kernel(table_ref, row_ref, col_ref, high_ref, low_ref, row_waves_ref, col_waves_ref, picked_ref):
    for q in range(row_ref.shape[0]):
        row_high, row_low = waves(table_ref[...], row_ref[q : q + 1, :])
        col_high, col_low = waves(table_ref[...], col_ref[q : q + 1, :])
        row_waves_ref[q, 0:pair, :] = row_high
        row_waves_ref[q, pair:, :] = row_low
        col_waves_ref[q, 0:pair, :] = col_high
        col_waves_ref[q, pair:, :] = col_low
        at = slice(q * pair, (q + 1) * pair)
        high = high_ref[:, at]
        both = jnp.concatenate([high, low_ref[:, at]], axis=1)
        half = dot(both, jnp.concatenate([row_high, row_high], axis=0), ((1,), (0,)))
        half += dot(high, row_low, ((1,), (0,)))
        picked_ref[q : q + 1, :] = jnp.sum(
            half * (col_high.astype(f32) + col_low.astype(f32)), axis=0, keepdims=True
        )


def pick(table, rows, cols, high, low):
    tiles = rows.shape[0]
    return pl.pallas_call(
        pick_kernel,
        out_shape=(
            jax.ShapeDtypeStruct((tiles, 2 * pair, pair), bf16),
            jax.ShapeDtypeStruct((tiles, 2 * pair, pair), bf16),
            jax.ShapeDtypeStruct((tiles, pair), f32),
        ),
        compiler_params=pltpu.CompilerParams(vmem_limit_bytes=40 * 2**20),
        name="pick",
    )(table, rows, cols, high, low)


def momentum_kernel(message_ref, momentum_ref, row_waves_ref, col_waves_ref, out_ref, mid_ref):
    owners, tall, _ = message_ref.shape
    rows = out_ref.shape[0]
    total = decay_rate * momentum_ref[...]
    for source in range(owners):
        power = message_ref[source, rows:tall, :].astype(jnp.int32)[0:1, :].astype(f32)
        total += message_ref[source, 0:rows, :].astype(jnp.int32).astype(f32) * jnp.exp2(power)
    mid_ref[0:rows, :] = total
    mid_ref[rows:, :] = jnp.zeros((mid_ref.shape[0] - rows, pair), f32)
    highest = functools.partial(lax.dot_general, precision=lax.Precision.HIGHEST, preferred_element_type=f32)
    for q in range(row_waves_ref.shape[0]):
        tile = mid_ref[q * pair : (q + 1) * pair, :]
        half = highest(tile, row_waves_ref[q], (((0,), (0,)), ((), ())))
        picked = jnp.sum(half * col_waves_ref[q], axis=0, keepdims=True)
        sent = highest(row_waves_ref[q], picked * col_waves_ref[q], (((1,), (1,)), ((), ())))
        left = min(pair, rows - q * pair)
        out_ref[q * pair : q * pair + left, :] = (tile - sent)[:left]


def new_momentum_of(message, momentum, row_waves, col_waves):
    tiles = row_waves.shape[0]
    return pl.pallas_call(
        momentum_kernel,
        out_shape=jax.ShapeDtypeStruct(momentum.shape, f32),
        scratch_shapes=[pltpu.VMEM((tiles * pair, pair), f32)],
        compiler_params=pltpu.CompilerParams(vmem_limit_bytes=40 * 2**20),
        name="momentum_step",
    )(message, momentum, row_waves, col_waves)


def weight_kernel(nodes, total_ref, row_waves_ref, col_waves_ref, weight_ref, out_ref):
    for q in range(total_ref.shape[0]):
        at = slice(q * pair, (q + 1) * pair)
        mean = total_ref[q : q + 1, :] / nodes
        col_waves = col_waves_ref[q, 0:pair, :].astype(f32) + col_waves_ref[q, pair:, :].astype(f32)
        high, low = split2(mean * col_waves)
        row_high, row_low = row_waves_ref[q, 0:pair, :], row_waves_ref[q, pair:, :]
        field = dot(
            jnp.concatenate([row_high, row_low], axis=1), jnp.concatenate([high, high], axis=1), ((1,), (1,))
        )
        field += dot(row_high, low, ((1,), (1,)))
        out_ref[at, :] = (weight_ref[at, :].astype(f32) - learn_rate * jnp.tanh(field)).astype(bf16)


def new_weight_of(total, row_waves, col_waves, weight, nodes):
    return pl.pallas_call(
        functools.partial(weight_kernel, nodes),
        out_shape=jax.ShapeDtypeStruct(weight.shape, bf16),
        compiler_params=pltpu.CompilerParams(vmem_limit_bytes=40 * 2**20),
        name="weight_step",
    )(total, row_waves, col_waves, weight)


def on_device(hidden, gain, cotangent, weight, momentum, indices):
    nodes, owners = lax.axis_size("node"), lax.axis_size("local")
    node, local = lax.axis_index("node"), lax.axis_index("local")
    features = hidden.shape[1]
    own_rows, head = weight.shape
    table = pair_table()
    blocks = indices.size
    row_of, col_of = indices // side, indices % side

    eighth = own_rows // 8
    part = (node // 8) * 2 + node % 2
    with jax.named_scope("weight_part"):
        piece = lax.dynamic_slice_in_dim(weight, part * eighth, eighth, axis=0)
        spots = jnp.concatenate([row_of.reshape(-1), col_of.reshape(-1)]).astype(bf16).reshape(-1, head)
        spots = jnp.pad(spots, ((0, 8 - spots.shape[0]), (0, 0)))
        piece = jnp.concatenate([piece, spots], axis=0)
    with jax.named_scope("weight_over_y"):
        other = hop(piece, lambda x, y, z, c: (x, (y + 4) % 8, z, c))
        upper = local % 2
        two = jnp.where(upper == 0, jnp.stack([piece, other]), jnp.stack([other, piece]))
    with jax.named_scope("weight_over_z"):
        gathered = lax.all_to_all(
            jnp.broadcast_to(two[None], (8,) + two.shape), "local", 0, 0, axis_index_groups=z_groups
        )
        gathered = gathered.reshape(owners, eighth + 8, head)

    message, high, low = front(hidden, gain[None, :], cotangent, owners)
    with jax.named_scope("gradient_exchange"):
        arrived = lax.all_to_all(message, "local", 0, 0)

    spare = (-blocks) % pair
    tiles = (blocks + spare) // pair
    own_at = jnp.pad(indices.reshape(-1), (0, spare)).reshape(tiles, pair)
    quarter = 2 * side * (jnp.arange(pair, dtype=jnp.int32) // side)[None, :]
    block_in = (jnp.arange(pair, dtype=jnp.int32) // 32)[None, :]
    place = lambda rows, cols: (rows + side * (block_in // 2), cols + side * (block_in % 2))
    own_row, own_col = place(own_at // side, own_at % side)
    own_momentum = momentum[0]
    padded = jnp.pad(own_momentum, ((0, tiles * pair - own_rows), (0, 0)))
    row_waves, col_waves, decayed = own_waves(table, own_row, own_col, padded)
    decayed = lax.dynamic_update_slice(
        jnp.zeros((owners * blocks,), f32), decayed.reshape(-1)[:blocks], (local * blocks,)
    ).reshape(-1, pair)

    spots = gathered[:, eighth:, :].reshape(owners, -1)[:, : 2 * blocks].astype(jnp.int32)
    all_row, all_col = place(spots[:, :blocks].reshape(-1, pair), spots[:, blocks:].reshape(-1, pair))
    all_row_waves, all_col_waves, picked = pick(table, all_row, all_col, high, low)
    with jax.named_scope("coefficients"):
        total = picked + decayed
        total = jnp.sum(lax.all_gather(total, "node", axis_index_groups=core_groups), axis=0)
        total = total + hop(total, lambda x, y, z, c: (x, y ^ 1, z, c))
        total = total + hop(total, lambda x, y, z, c: (x, y ^ 2, z, c))
        total = total + hop(total, lambda x, y, z, c: (x, y ^ 4, z, c))
        spread = lambda v, n: jnp.broadcast_to(v[None], (n,) + v.shape)
        total = jnp.sum(lax.all_to_all(spread(total, 8), "local", 0, 0, axis_index_groups=z_groups), axis=0)
        total = jnp.sum(lax.all_to_all(spread(total, 4), "node", 0, 0, axis_index_groups=x_groups), axis=0)

    with jax.named_scope("weight_over_x"):
        quarter = gathered[:, :eighth, :]
        half = lax.all_to_all(spread(quarter, 4), "node", 0, 0, axis_index_groups=x_groups)
    with jax.named_scope("weight_over_core"):
        full = lax.all_gather(half, "node", axis_index_groups=core_groups)
        full = jnp.transpose(full, (2, 1, 0, 3, 4)).reshape(features, head)

    wide = hidden.astype(f32)
    scale = lax.rsqrt(jnp.mean(wide * wide, axis=1, keepdims=True) + epsilon)
    gained = gain * dot(cotangent, full, ((1,), (1,)))
    back = scale * gained - wide * scale**3 * jnp.mean(wide * gained, axis=1, keepdims=True)
    input_grad = back.astype(bf16)

    new_momentum = new_momentum_of(arrived, own_momentum, row_waves, col_waves)[None]
    new_weight = new_weight_of(total, all_row_waves, all_col_waves, full, nodes)
    return (new_weight, new_momentum, input_grad)


def solution(mesh):
    return jax.shard_map(
        on_device,
        mesh=mesh,
        in_specs=(
            P(("node", "local"), None),
            P(),
            P(("node", "local"), None),
            P("local", None),
            P("node", "local", None),
            P("local", None),
        ),
        out_specs=(P(), P("node", "local", None), P(("node", "local"), None)),
        check_vma=False,
    )
```

```python
import functools

import jax
import jax.numpy as jnp
from jax import lax
from jax.experimental import pallas as pl
from jax.experimental.pallas import tpu as pltpu
from jax.sharding import PartitionSpec as P

epsilon = 1e-06
decay_rate = 0.9
learn_rate = 0.01
side = 64
pair = 128
f32 = jnp.float32
bf16 = jnp.bfloat16
kernel_room = pltpu.CompilerParams(vmem_limit_bytes=24 * 2**20)
small = pl.CostEstimate(flops=1, bytes_accessed=1, transcendentals=0)

z_groups = [[2 * z + h for z in range(8)] for h in range(2)]
x_groups = [[8 * x + r for x in range(4)] for r in range(8)]
x_core_groups = [[8 * x + 2 * r + c for x in range(4) for c in range(2)] for r in range(4)]


def whole_mesh(move):
    def index(x, y, z, core):
        return ((x * 4 + y % 4) * 2 + core) * 16 + z * 2 + y // 4

    places = [(x, y, z, c) for x in range(4) for y in range(8) for z in range(8) for c in range(2)]
    sizes = (4, 8, 8, 2)
    wrap = lambda place: [at % size for at, size in zip(place, sizes)]
    return [(index(*place), index(*wrap(move(*place)))) for place in places]


def hop(value, move):
    return lax.ppermute(value, ("node", "local"), whole_mesh(move))


def over_z(value):
    return lax.all_to_all(value, "local", 0, 0, axis_index_groups=z_groups)


def dct_table():
    freq = jnp.arange(side, dtype=f32)[:, None]
    place = jnp.arange(side, dtype=f32)[None, :]
    wave = jnp.cos(jnp.pi * (2.0 * place + 1.0) * freq / (2.0 * side))
    norm_row = jnp.where(freq == 0.0, jnp.sqrt(1.0 / side), jnp.sqrt(2.0 / side))
    return wave * norm_row


def split2(value):
    high = value.astype(bf16)
    return high, (value - high.astype(f32)).astype(bf16)


def pair_tables():
    table = dct_table()
    empty = jnp.zeros_like(table)
    wide = jnp.block([[table, empty], [empty, table]])
    high = lax.reduce_precision(wide, exponent_bits=8, mantissa_bits=7)
    low = wide - high
    turned = jnp.concatenate([high.T, low.T], axis=0).astype(bf16)
    return turned, jnp.concatenate([high, low], axis=1).astype(bf16)


def dot(a, b, dims):
    return lax.dot_general(a, b, (dims, ((), ())), preferred_element_type=f32)


def from_hbm(value):
    return pltpu.with_memory_space_constraint(value, pltpu.HBM)


in_hbm = pl.BlockSpec(memory_space=pltpu.HBM)
in_vmem = pl.BlockSpec(memory_space=pltpu.VMEM)
in_smem = pl.BlockSpec(memory_space=pltpu.SMEM)


def waves(table, spots):
    at = lax.broadcasted_iota(jnp.int32, (pair, pair), 0)
    chosen = jnp.where(at == spots, 1.0, 0.0).astype(bf16)
    both = dot(table, chosen, ((1,), (0,)))
    return both[:pair].astype(bf16), both[pair:].astype(bf16)


def coded(value):
    top = jnp.max(jnp.abs(value), axis=0, keepdims=True)
    power = jnp.clip(jnp.ceil(jnp.log2(top * (1.0 / 32000.0))), -120.0, 120.0)
    whole = jnp.round(value * jnp.exp2(-power)).astype(jnp.int32).astype(jnp.int16)
    return whole, jnp.broadcast_to(power.astype(jnp.int32), (16, pair)).astype(jnp.int16)


def decoded(whole, power):
    return whole.astype(jnp.int32).astype(f32) * jnp.exp2(power.astype(jnp.int32)[0:1, :].astype(f32))


def front_kernel(
    hidden_ref, gain_ref, cot_ref, message_out_ref, high_out_ref, low_out_ref,
    message_ref, high_ref, low_ref, message_done, high_done, low_done,
):
    wide = hidden_ref[...].astype(f32)
    features = wide.shape[1]
    lines, _, tall, _ = message_ref.shape
    rows = tall - 16
    scale = lax.rsqrt(jnp.sum(wide * wide, axis=1, keepdims=True) * (1.0 / features) + epsilon)
    cot = cot_ref[...]
    copies = []
    for line in range(lines):
        at = slice(line * 2 * rows, (line + 1) * 2 * rows)
        normed = (hidden_ref[:, at].astype(f32) * scale * gain_ref[:, at]).astype(bf16)
        term = dot(normed, cot, ((0,), (0,)))
        high_ref[line], low_ref[line] = split2(term)
        for half in range(2):
            own = term[half * rows : (half + 1) * rows]
            message_ref[line, half, 0:rows, :], message_ref[line, half, rows:tall, :] = coded(own)
        for source, target, done in (
            (message_ref, message_out_ref, message_done),
            (high_ref, high_out_ref, high_done),
            (low_ref, low_out_ref, low_done),
        ):
            copies.append(pltpu.make_async_copy(source.at[line], target.at[line], done.at[line]))
            copies[-1].start()
    for copy in copies:
        copy.wait()


def front(hidden, gain, cot, owners):
    tokens, features = hidden.shape
    lines, rows = owners // 2, features // owners
    outs = (
        pltpu.HBM((lines, 2, rows + 16, pair), jnp.int16),
        pltpu.HBM((lines, 2 * rows, pair), bf16),
        pltpu.HBM((lines, 2 * rows, pair), bf16),
    )
    return pl.pallas_call(
        front_kernel,
        out_shape=outs,
        in_specs=[in_vmem] * 3,
        out_specs=(in_hbm,) * 3,
        scratch_shapes=[pltpu.VMEM(out.shape, out.dtype) for out in outs]
        + [pltpu.SemaphoreType.DMA((lines,))] * 3,
        compiler_params=kernel_room,
        cost_estimate=small,
        name="front",
    )(hidden, gain, cot)


def own_kernel(table_ref, row_ref, col_ref, momentum_ref, row_waves_ref, col_waves_ref, picked_ref):
    for q in range(row_ref.shape[0]):
        row_high, row_low = waves(table_ref[...], row_ref[q : q + 1, :])
        col_high, col_low = waves(table_ref[...], col_ref[q : q + 1, :])
        row_waves = row_high.astype(f32) + row_low.astype(f32)
        col_waves = col_high.astype(f32) + col_low.astype(f32)
        row_waves_ref[q] = row_waves
        col_waves_ref[q] = col_waves
        tile = decay_rate * momentum_ref[q * pair : min((q + 1) * pair, momentum_ref.shape[0]), :]
        short = pair - tile.shape[0]
        if short:
            tile = jnp.concatenate([tile, jnp.zeros((short, pair), f32)], axis=0)
        half = lax.dot_general(
            tile, row_waves, (((0,), (0,)), ((), ())), precision=lax.Precision.HIGHEST, preferred_element_type=f32
        )
        picked_ref[q : q + 1, :] = jnp.sum(half * col_waves, axis=0, keepdims=True)


def own_waves(table, rows, cols, momentum):
    tiles = rows.shape[0]
    return pl.pallas_call(
        own_kernel,
        out_shape=(
            jax.ShapeDtypeStruct((tiles, pair, pair), f32),
            jax.ShapeDtypeStruct((tiles, pair, pair), f32),
            jax.ShapeDtypeStruct((tiles, pair), f32),
        ),
        cost_estimate=small,
        name="own_waves",
    )(table, rows, cols, momentum)


def pack_kernel(upper_ref, mine_ref, other_ref, _, out_ref):
    eighth = mine_ref.shape[0] - 16
    mine, other = mine_ref[...].astype(f32), other_ref[...].astype(f32)
    first = upper_ref[0] == 0
    low = jnp.where(first, mine[:eighth], other[:eighth])
    high = jnp.where(first, other[:eighth], mine[:eighth])
    packed = jnp.concatenate([low, high, mine[eighth:] + other[eighth:]], axis=0).astype(bf16)
    for target in range(out_ref.shape[0]):
        out_ref[target] = packed


def pack(upper, mine, other, after):
    return pl.pallas_call(
        pack_kernel,
        out_shape=jax.ShapeDtypeStruct((8, 2 * mine.shape[0] - 16, pair), bf16),
        in_specs=[in_smem, in_vmem, in_vmem, pl.BlockSpec(memory_space=pl.ANY)],
        cost_estimate=small,
        name="pack",
    )(upper[None], mine, other, after)


def block_offsets(spots):
    block_in = lax.broadcasted_iota(jnp.int32, spots.shape, 1) // 32
    is_row = lax.broadcasted_iota(jnp.int32, spots.shape, 0) % 16 < 8
    return spots + side * jnp.where(is_row, block_in // 2, block_in % 2).astype(spots.dtype)


def pick_kernel(
    table_ref, spots_ref, high_in_ref, low_in_ref, decayed_ref, picked_ref, high_ref, low_ref, high_done, low_done
):
    lines, tall, _ = spots_ref.shape
    tiles = picked_ref.shape[0]
    each = tiles // lines
    arrivals = []
    for line in range(lines):
        arrivals.append(pltpu.make_async_copy(high_in_ref.at[line], high_ref.at[line], high_done.at[line]))
        arrivals.append(pltpu.make_async_copy(low_in_ref.at[line], low_ref.at[line], low_done.at[line]))
        arrivals[-2].start()
        arrivals[-1].start()
    spots = [spots_ref[line, tall - 16 : tall, :].astype(f32) for line in range(lines)]
    spots = jnp.transpose(block_offsets(jnp.concatenate(spots, axis=0)))
    across = lax.broadcasted_iota(jnp.int32, (pair, pair), 1)
    lane = across.astype(f32)
    table = table_ref[...]
    picked = jnp.zeros((pair, pair), f32)
    for line in range(lines):
        arrivals[2 * line].wait()
        arrivals[2 * line + 1].wait()
        for tile in range(each):
            chosen = []
            for at in (line * 16 + tile, line * 16 + 8 + tile):
                chosen.append(jnp.where(lane == spots[:, at : at + 1], 1.0, 0.0).astype(bf16))
            rows = dot(chosen[0], table, ((1,), (0,))).astype(bf16)
            cols = dot(chosen[1], table, ((1,), (0,)))
            at = slice(tile * pair, (tile + 1) * pair)
            high = high_ref[line, at, :]
            half = dot(rows, jnp.concatenate([high, high], axis=0), ((1,), (0,)))
            half += dot(rows[:, :pair], low_ref[line, at, :], ((1,), (0,)))
            found = jnp.sum(half * (cols[:, :pair] + cols[:, pair:]), axis=1, keepdims=True)
            picked = jnp.where(across == line * each + tile, found, picked)
    picked_ref[...] = jnp.transpose(picked)[:tiles] + decayed_ref[...]


def pick(table, spots, high, low, decayed):
    lines = spots.shape[0]
    return pl.pallas_call(
        pick_kernel,
        out_shape=jax.ShapeDtypeStruct(decayed.shape, f32),
        in_specs=[in_vmem, in_vmem, in_hbm, in_hbm, in_vmem],
        scratch_shapes=[pltpu.VMEM(high.shape, bf16)] * 2 + [pltpu.SemaphoreType.DMA((lines,))] * 2,
        compiler_params=kernel_room,
        cost_estimate=small,
        name="pick",
    )(table, spots, from_hbm(high), from_hbm(low), decayed)


def middle_kernel(upper_ref, message_ref, total_ref, own_ref, rest_out_ref, spread_ref, rest_ref, rest_done):
    sources, halves, tall, _ = message_ref.shape
    rows = own_ref.shape[0]
    sums = []
    for half in range(halves):
        term = jnp.zeros(own_ref.shape, f32)
        for source in range(sources):
            term += decoded(message_ref[source, half, 0:rows, :], message_ref[source, half, rows:tall, :])
        sums.append(term)
    first = upper_ref[0] == 0
    own_ref[...] = jnp.where(first, sums[0], sums[1])
    rest_ref[0:rows, :], rest_ref[rows:tall, :] = coded(jnp.where(first, sums[1], sums[0]))
    copy = pltpu.make_async_copy(rest_ref, rest_out_ref, rest_done)
    copy.start()
    for source in range(sources):
        spread_ref[source] = total_ref[...]
    copy.wait()


def middle(message, upper, total):
    sources, _, tall, _ = message.shape
    return pl.pallas_call(
        middle_kernel,
        out_shape=(
            jax.ShapeDtypeStruct((tall - 16, pair), f32),
            pltpu.HBM((tall, pair), jnp.int16),
            jax.ShapeDtypeStruct((sources,) + total.shape, f32),
        ),
        out_specs=(in_vmem, in_hbm, in_vmem),
        scratch_shapes=[pltpu.VMEM((tall, pair), jnp.int16), pltpu.SemaphoreType.DMA],
        in_specs=[in_smem, in_vmem, in_vmem],
        compiler_params=kernel_room,
        cost_estimate=small,
        name="middle",
    )(upper[None], message, total)


def momentum_kernel(sum_ref, rest_ref, momentum_ref, row_waves_ref, col_waves_ref, out_ref, mid_ref):
    rows = out_ref.shape[0]
    total = decay_rate * momentum_ref[...] + sum_ref[...]
    mid_ref[0:rows, :] = total + decoded(rest_ref[0:rows, :], rest_ref[rows:, :])
    mid_ref[rows:, :] = jnp.zeros((mid_ref.shape[0] - rows, pair), f32)
    highest = functools.partial(lax.dot_general, precision=lax.Precision.HIGHEST, preferred_element_type=f32)
    for q in range(row_waves_ref.shape[0]):
        tile = mid_ref[q * pair : (q + 1) * pair, :]
        half = highest(tile, row_waves_ref[q], (((0,), (0,)), ((), ())))
        picked = jnp.sum(half * col_waves_ref[q], axis=0, keepdims=True)
        sent = highest(row_waves_ref[q], picked * col_waves_ref[q], (((1,), (1,)), ((), ())))
        left = min(pair, rows - q * pair)
        out_ref[q * pair : q * pair + left, :] = (tile - sent)[:left]


def new_momentum_of(own_sum, rest, momentum, row_waves, col_waves):
    tiles = row_waves.shape[0]
    return pl.pallas_call(
        momentum_kernel,
        out_shape=jax.ShapeDtypeStruct(momentum.shape, f32),
        scratch_shapes=[pltpu.VMEM((tiles * pair, pair), f32)],
        compiler_params=kernel_room,
        cost_estimate=small,
        name="momentum_step",
    )(own_sum, rest, momentum, row_waves, col_waves)


def weight_rows(parts_ref, line):
    parts = [parts_ref[part, line].astype(f32) for part in range(parts_ref.shape[0])]
    eighth = parts[0].shape[0] // 2
    return jnp.concatenate([p[:eighth] for p in parts] + [p[eighth:] for p in parts], axis=0)


def weight_kernel(nodes, table_ref, spots_ref, total_ref, parts_ref, out_ref):
    lines, tall, _ = spots_ref.shape
    total = total_ref[0]
    for part in range(1, total_ref.shape[0]):
        total += total_ref[part]
    total = total / nodes
    each = total.shape[0] // lines
    table = table_ref[...]
    for line in range(lines):
        weight = weight_rows(parts_ref, line)
        spots = block_offsets(spots_ref[line, tall - 16 : tall, :].astype(f32).astype(jnp.int32))
        for tile in range(each):
            q = line * each + tile
            row_high, row_low = waves(table, spots[tile : tile + 1])
            col_high, col_low = waves(table, spots[8 + tile : 9 + tile])
            high, low = split2(total[q : q + 1, :] * (col_high.astype(f32) + col_low.astype(f32)))
            field = dot(
                jnp.concatenate([row_high, row_low], axis=1), jnp.concatenate([high, high], axis=1), ((1,), (1,))
            )
            field += dot(row_high, low, ((1,), (1,)))
            fresh = weight[tile * pair : (tile + 1) * pair] - learn_rate * jnp.tanh(field)
            out_ref[q * pair : (q + 1) * pair, :] = fresh.astype(bf16)


def new_weight_of(table, spots, total, parts, nodes):
    return pl.pallas_call(
        functools.partial(weight_kernel, nodes),
        out_shape=jax.ShapeDtypeStruct((total.shape[1] * pair, pair), bf16),
        compiler_params=kernel_room,
        cost_estimate=small,
        name="weight_step",
    )(table, spots, total, parts)


def input_kernel(hidden_ref, gain_ref, cot_ref, parts_ref, out_ref, gained_ref):
    features = hidden_ref.shape[1]
    wide = hidden_ref[...].astype(f32)
    scale = lax.rsqrt(jnp.sum(wide * wide, axis=1, keepdims=True) * (1.0 / features) + epsilon)
    cot = cot_ref[...]
    lines = parts_ref.shape[1]
    step = features // lines
    along = jnp.zeros(scale.shape, f32)
    for piece in range(lines):
        at = slice(piece * step, (piece + 1) * step)
        weight = weight_rows(parts_ref, piece).astype(bf16)
        gained = gain_ref[:, at] * dot(cot, weight, ((1,), (1,)))
        gained_ref[:, at] = gained
        along += jnp.sum(hidden_ref[:, at].astype(f32) * gained, axis=1, keepdims=True)
    factor = scale**3 * (along * (1.0 / features))
    for piece in range(lines):
        at = slice(piece * step, (piece + 1) * step)
        out_ref[:, at] = (scale * gained_ref[:, at] - hidden_ref[:, at].astype(f32) * factor).astype(bf16)


def input_grad_of(hidden, gain, cot, parts):
    return pl.pallas_call(
        input_kernel,
        out_shape=jax.ShapeDtypeStruct(hidden.shape, bf16),
        scratch_shapes=[pltpu.VMEM(hidden.shape, f32)],
        compiler_params=kernel_room,
        cost_estimate=small,
        name="input_gradient",
    )(hidden, gain, cot, parts)


def on_device(hidden, gain, cotangent, weight, momentum, indices):
    nodes, owners = lax.axis_size("node"), lax.axis_size("local")
    node, local = lax.axis_index("node"), lax.axis_index("local")
    features = hidden.shape[1]
    own_rows, head = weight.shape
    turned, table = pair_tables()
    blocks = indices.size
    row_of, col_of = indices // side, indices % side

    upper = local % 2
    eighth = own_rows // 8
    part = (node // 8) * 2 + node % 2
    with jax.named_scope("weight_part"):
        piece = lax.dynamic_slice_in_dim(weight, part * eighth, eighth, axis=0)
        at_half = lambda spots: lax.dynamic_update_slice(
            jnp.zeros((8 * pair,), jnp.int32), spots.reshape(-1), (upper * blocks,)
        ).reshape(8, pair)
        piece = jnp.concatenate([piece, at_half(row_of).astype(bf16), at_half(col_of).astype(bf16)], axis=0)
    with jax.named_scope("weight_over_y"):
        other = hop(piece, lambda x, y, z, c: (x, (y + (2 if y in (2, 3, 6, 7) else 6)) % 8, z, c))

    spare = (-blocks) % pair
    tiles = (blocks + spare) // pair
    own_at = jnp.pad(indices.reshape(-1), (0, spare)).reshape(tiles, pair)
    block_in = (jnp.arange(pair, dtype=jnp.int32) // 32)[None, :]
    place = lambda rows, cols: (rows + side * (block_in // 2), cols + side * (block_in % 2))
    own_row, own_col = place(own_at // side, own_at % side)
    own_momentum = momentum[0]
    row_waves, col_waves, decayed = own_waves(turned, own_row, own_col, own_momentum)
    decayed = lax.dynamic_update_slice(
        jnp.zeros((owners * blocks,), f32), decayed.reshape(-1)[:blocks], (local * blocks,)
    ).reshape(-1, pair)

    with jax.named_scope("weight_over_z"):
        gathered = over_z(pack(upper, piece, other, decayed))

    message, high, low = front(hidden, gain[None, :], cotangent, owners)
    with jax.named_scope("gradient_exchange"):
        arrived = over_z(message)

    total = pick(table, gathered, high, low, decayed)
    with jax.named_scope("coefficients"):
        total = total + hop(total, lambda x, y, z, c: (x, y, z, 1 - c))
        total = total + hop(total, lambda x, y, z, c: (x, y ^ 1, z, c))
        total = total + hop(total, lambda x, y, z, c: (x, ((y + 1) ^ 1) - 1, z, c))
        total = total + hop(total, lambda x, y, z, c: (x, y ^ 3 if y in (0, 3, 4, 7) else 7 - y, z, c))
    own_sum, rest, spread = middle(arrived, upper, total)
    with jax.named_scope("coefficients_over_z"):
        totals = jnp.sum(over_z(spread), axis=0)
    with jax.named_scope("coefficients_over_x"):
        totals = jnp.broadcast_to(totals[None], (4,) + totals.shape)
        totals = lax.all_to_all(totals, "node", 0, 0, axis_index_groups=x_groups)
    with jax.named_scope("gradient_over_y"):
        rest = hop(rest, lambda x, y, z, c: (x, (y + 4) % 8, z, c))

    with jax.named_scope("weight_over_x_and_core"):
        parts = lax.all_gather(gathered[:, : 2 * eighth, :], "node", axis_index_groups=x_core_groups)

    input_grad = input_grad_of(hidden, gain[None, :], cotangent, parts)
    new_momentum = new_momentum_of(own_sum, rest, own_momentum, row_waves, col_waves)[None]
    new_weight = new_weight_of(turned, gathered, totals, parts, nodes)
    return (new_weight, new_momentum, input_grad)


def solution(mesh):
    return jax.shard_map(
        on_device,
        mesh=mesh,
        in_specs=(
            P(("node", "local"), None),
            P(),
            P(("node", "local"), None),
            P("local", None),
            P("node", "local", None),
            P("local", None),
        ),
        out_specs=(P(), P("node", "local", None), P(("node", "local"), None)),
        check_vma=False,
    )
```

```python
import functools

import jax
import jax.numpy as jnp
from jax import lax
from jax.experimental import pallas as pl
from jax.experimental.pallas import tpu as pltpu
from jax.sharding import PartitionSpec as P

epsilon = 1e-06
decay_rate = 0.9
learn_rate = 0.01
side = 64
pair = 128
f32 = jnp.float32
bf16 = jnp.bfloat16
kernel_room = pltpu.CompilerParams(vmem_limit_bytes=24 * 2**20)
small = pl.CostEstimate(flops=1, bytes_accessed=1, transcendentals=0)

z_groups = [[2 * z + h for z in range(8)] for h in range(2)]
x_groups = [[8 * x + r for x in range(4)] for r in range(8)]
x_core_groups = [[8 * x + 2 * r + c for x in range(4) for c in range(2)] for r in range(4)]


def whole_mesh(move):
    def index(x, y, z, core):
        return ((x * 4 + y % 4) * 2 + core) * 16 + z * 2 + y // 4

    places = [(x, y, z, c) for x in range(4) for y in range(8) for z in range(8) for c in range(2)]
    sizes = (4, 8, 8, 2)
    wrap = lambda place: [at % size for at, size in zip(place, sizes)]
    return [(index(*place), index(*wrap(move(*place)))) for place in places]


def hop(value, move):
    return lax.ppermute(value, ("node", "local"), whole_mesh(move))


def over_z(value):
    return lax.all_to_all(value, "local", 0, 0, axis_index_groups=z_groups)


def dct_table():
    freq = jnp.arange(side, dtype=f32)[:, None]
    place = jnp.arange(side, dtype=f32)[None, :]
    wave = jnp.cos(jnp.pi * (2.0 * place + 1.0) * freq / (2.0 * side))
    norm_row = jnp.where(freq == 0.0, jnp.sqrt(1.0 / side), jnp.sqrt(2.0 / side))
    return wave * norm_row


def split2(value):
    high = value.astype(bf16)
    return high, (value - high.astype(f32)).astype(bf16)


def wave_table():
    turned = dct_table().T
    high = lax.reduce_precision(turned, exponent_bits=8, mantissa_bits=7)
    low = turned - high
    empty = jnp.zeros_like(turned)
    return jnp.block([[high, empty], [low, empty], [empty, high], [empty, low]]).astype(bf16)


def dot(a, b, dims):
    return lax.dot_general(a, b, (dims, ((), ())), preferred_element_type=f32)


def from_hbm(value):
    return pltpu.with_memory_space_constraint(value, pltpu.HBM)


in_hbm = pl.BlockSpec(memory_space=pltpu.HBM)
in_vmem = pl.BlockSpec(memory_space=pltpu.VMEM)
in_smem = pl.BlockSpec(memory_space=pltpu.SMEM)


def waves(table, spots):
    tiles = spots.shape[0] // 2
    rows = jnp.concatenate([spots[at : at + 1] for at in range(tiles)], axis=1)
    cols = jnp.concatenate([spots[at : at + 1] for at in range(tiles, 2 * tiles)], axis=1)
    wide = (side, tiles * pair)
    at = lax.broadcasted_iota(jnp.int32, wide, 0)
    chosen = jnp.concatenate([jnp.where(at == rows, 1.0, 0.0), jnp.where(at == cols, 1.0, 0.0)], axis=0)
    found = dot(table, chosen.astype(bf16), ((1,), (0,)))
    block = lax.broadcasted_iota(jnp.int32, wide, 1) // 32 % 4

    def placed(value, second):
        return jnp.concatenate([jnp.where(second, 0.0, value), jnp.where(second, value, 0.0)], axis=0)

    below, right = block >= 2, block % 2 == 1
    row_high = placed(found[:side], below).astype(bf16)
    row_low = placed(found[side : 2 * side], below).astype(bf16)
    return row_high, row_low, placed(found[2 * side : 3 * side] + found[3 * side :], right)


def coded(value):
    top = jnp.max(jnp.abs(value), axis=0, keepdims=True)
    power = jnp.clip(jnp.ceil(jnp.log2(top * (1.0 / 32000.0))), -120.0, 120.0)
    whole = jnp.round(value * jnp.exp2(-power)).astype(jnp.int32).astype(jnp.int16)
    return whole, jnp.broadcast_to(power.astype(jnp.int32), (16, pair)).astype(jnp.int16)


def decoded(whole, power):
    return whole.astype(jnp.int32).astype(f32) * jnp.exp2(power.astype(jnp.int32)[0:1, :].astype(f32))


def front_kernel(
    hidden_ref, gain_ref, cot_ref, message_out_ref, high_out_ref, low_out_ref,
    message_ref, high_ref, low_ref, message_done, high_done, low_done,
):
    wide = hidden_ref[...].astype(f32)
    features = wide.shape[1]
    lines, _, tall, _ = message_ref.shape
    rows = tall - 16
    scale = lax.rsqrt(jnp.sum(wide * wide, axis=1, keepdims=True) * (1.0 / features) + epsilon)
    cot = cot_ref[...]
    copies = []
    for line in range(lines):
        at = slice(line * 2 * rows, (line + 1) * 2 * rows)
        normed = (hidden_ref[:, at].astype(f32) * scale * gain_ref[:, at]).astype(bf16)
        term = dot(normed, cot, ((0,), (0,)))
        high_ref[line], low_ref[line] = split2(dot(cot, normed, ((0,), (0,))))
        for half in range(2):
            own = term[half * rows : (half + 1) * rows]
            message_ref[line, half, 0:rows, :], message_ref[line, half, rows:tall, :] = coded(own)
        for source, target, done in (
            (message_ref, message_out_ref, message_done),
            (high_ref, high_out_ref, high_done),
            (low_ref, low_out_ref, low_done),
        ):
            copies.append(pltpu.make_async_copy(source.at[line], target.at[line], done.at[line]))
            copies[-1].start()
    for copy in copies:
        copy.wait()


def front(hidden, gain, cot, owners):
    tokens, features = hidden.shape
    lines, rows = owners // 2, features // owners
    outs = (
        pltpu.HBM((lines, 2, rows + 16, pair), jnp.int16),
        pltpu.HBM((lines, pair, 2 * rows), bf16),
        pltpu.HBM((lines, pair, 2 * rows), bf16),
    )
    return pl.pallas_call(
        front_kernel,
        out_shape=outs,
        in_specs=[in_vmem] * 3,
        out_specs=(in_hbm,) * 3,
        scratch_shapes=[pltpu.VMEM(out.shape, out.dtype) for out in outs]
        + [pltpu.SemaphoreType.DMA((lines,))] * 3,
        compiler_params=kernel_room,
        cost_estimate=small,
        name="front",
    )(hidden, gain, cot)


def own_kernel(table_ref, spots_ref, momentum_ref, row_waves_ref, col_waves_ref, picked_ref):
    row_high, row_low, col_waves = waves(table_ref[...], spots_ref[...])
    row_waves = row_high.astype(f32) + row_low.astype(f32)
    for q in range(picked_ref.shape[0]):
        at = slice(q * pair, (q + 1) * pair)
        row_waves_ref[q] = row_waves[:, at]
        col_waves_ref[q] = col_waves[:, at]
        tile = decay_rate * momentum_ref[q * pair : min((q + 1) * pair, momentum_ref.shape[0]), :]
        short = pair - tile.shape[0]
        if short:
            tile = jnp.concatenate([tile, jnp.zeros((short, pair), f32)], axis=0)
        half = lax.dot_general(
            tile,
            row_waves[:, at],
            (((0,), (0,)), ((), ())),
            precision=lax.Precision.HIGHEST,
            preferred_element_type=f32,
        )
        picked_ref[q : q + 1, :] = jnp.sum(half * col_waves[:, at], axis=0, keepdims=True)


def own_waves(table, spots, momentum):
    tiles = spots.shape[0] // 2
    return pl.pallas_call(
        own_kernel,
        out_shape=(
            jax.ShapeDtypeStruct((tiles, pair, pair), f32),
            jax.ShapeDtypeStruct((tiles, pair, pair), f32),
            jax.ShapeDtypeStruct((tiles, pair), f32),
        ),
        cost_estimate=small,
        name="own_waves",
    )(table, spots, momentum)


def pack_kernel(upper_ref, mine_ref, other_ref, _, out_ref):
    eighth = mine_ref.shape[0] - 16
    mine, other = mine_ref[...].astype(f32), other_ref[...].astype(f32)
    first = upper_ref[0] == 0
    low = jnp.where(first, mine[:eighth], other[:eighth])
    high = jnp.where(first, other[:eighth], mine[:eighth])
    packed = jnp.concatenate([low, high, mine[eighth:] + other[eighth:]], axis=0).astype(bf16)
    for target in range(out_ref.shape[0]):
        out_ref[target] = packed


def pack(upper, mine, other, after):
    return pl.pallas_call(
        pack_kernel,
        out_shape=jax.ShapeDtypeStruct((8, 2 * mine.shape[0] - 16, pair), bf16),
        in_specs=[in_smem, in_vmem, in_vmem, pl.BlockSpec(memory_space=pl.ANY)],
        cost_estimate=small,
        name="pack",
    )(upper[None], mine, other, after)


def line_spots(spots_ref, line, tiles):
    tall = spots_ref.shape[1]
    spots = spots_ref[line, tall - 16 : tall, :].astype(f32).astype(jnp.int32)
    return jnp.concatenate([spots[:tiles], spots[8 : 8 + tiles]], axis=0)


def pick_kernel(
    table_ref, spots_ref, high_in_ref, low_in_ref, decayed_ref, picked_ref, high_ref, low_ref, high_done, low_done
):
    lines = spots_ref.shape[0]
    tiles = picked_ref.shape[0]
    each = tiles // lines
    arrivals = []
    for line in range(lines):
        arrivals.append(pltpu.make_async_copy(high_in_ref.at[line], high_ref.at[line], high_done.at[line]))
        arrivals.append(pltpu.make_async_copy(low_in_ref.at[line], low_ref.at[line], low_done.at[line]))
        arrivals[-2].start()
        arrivals[-1].start()
    table = table_ref[...]
    for line in range(lines):
        row_high, row_low, col_waves = waves(table, line_spots(spots_ref, line, each))
        arrivals[2 * line].wait()
        arrivals[2 * line + 1].wait()
        for tile in range(each):
            q = line * each + tile
            at = slice(tile * pair, (tile + 1) * pair)
            high = high_ref[line, :, at]
            both = jnp.concatenate([high, low_ref[line, :, at]], axis=1)
            half = dot(both, jnp.concatenate([row_high[:, at], row_high[:, at]], axis=0), ((1,), (0,)))
            half += dot(high, row_low[:, at], ((1,), (0,)))
            picked_ref[q : q + 1, :] = decayed_ref[q : q + 1, :] + jnp.sum(
                half * col_waves[:, at], axis=0, keepdims=True
            )


def pick(table, spots, high, low, decayed):
    lines = spots.shape[0]
    return pl.pallas_call(
        pick_kernel,
        out_shape=jax.ShapeDtypeStruct(decayed.shape, f32),
        in_specs=[in_vmem, in_vmem, in_hbm, in_hbm, in_vmem],
        scratch_shapes=[pltpu.VMEM(high.shape, bf16)] * 2 + [pltpu.SemaphoreType.DMA((lines,))] * 2,
        compiler_params=kernel_room,
        cost_estimate=small,
        name="pick",
    )(table, spots, from_hbm(high), from_hbm(low), decayed)


def middle_kernel(upper_ref, message_ref, total_ref, own_ref, rest_out_ref, spread_ref, rest_ref, rest_done):
    sources, halves, tall, _ = message_ref.shape
    rows = own_ref.shape[0]
    sums = []
    for half in range(halves):
        term = jnp.zeros(own_ref.shape, f32)
        for source in range(sources):
            term += decoded(message_ref[source, half, 0:rows, :], message_ref[source, half, rows:tall, :])
        sums.append(term)
    first = upper_ref[0] == 0
    own_ref[...] = jnp.where(first, sums[0], sums[1])
    rest_ref[0:rows, :], rest_ref[rows:tall, :] = coded(jnp.where(first, sums[1], sums[0]))
    copy = pltpu.make_async_copy(rest_ref, rest_out_ref, rest_done)
    copy.start()
    for source in range(sources):
        spread_ref[source] = total_ref[...]
    copy.wait()


def middle(message, upper, total):
    sources, _, tall, _ = message.shape
    return pl.pallas_call(
        middle_kernel,
        out_shape=(
            jax.ShapeDtypeStruct((tall - 16, pair), f32),
            pltpu.HBM((tall, pair), jnp.int16),
            jax.ShapeDtypeStruct((sources,) + total.shape, f32),
        ),
        out_specs=(in_vmem, in_hbm, in_vmem),
        scratch_shapes=[pltpu.VMEM((tall, pair), jnp.int16), pltpu.SemaphoreType.DMA],
        in_specs=[in_smem, in_vmem, in_vmem],
        compiler_params=kernel_room,
        cost_estimate=small,
        name="middle",
    )(upper[None], message, total)


def momentum_kernel(sum_ref, rest_ref, momentum_ref, row_waves_ref, col_waves_ref, out_ref, mid_ref):
    rows = out_ref.shape[0]
    total = decay_rate * momentum_ref[...] + sum_ref[...]
    mid_ref[0:rows, :] = total + decoded(rest_ref[0:rows, :], rest_ref[rows:, :])
    mid_ref[rows:, :] = jnp.zeros((mid_ref.shape[0] - rows, pair), f32)
    highest = functools.partial(lax.dot_general, precision=lax.Precision.HIGHEST, preferred_element_type=f32)
    for q in range(row_waves_ref.shape[0]):
        tile = mid_ref[q * pair : (q + 1) * pair, :]
        half = highest(tile, row_waves_ref[q], (((0,), (0,)), ((), ())))
        picked = jnp.sum(half * col_waves_ref[q], axis=0, keepdims=True)
        sent = highest(row_waves_ref[q], picked * col_waves_ref[q], (((1,), (1,)), ((), ())))
        left = min(pair, rows - q * pair)
        out_ref[q * pair : q * pair + left, :] = (tile - sent)[:left]


def new_momentum_of(own_sum, rest, momentum, row_waves, col_waves):
    tiles = row_waves.shape[0]
    return pl.pallas_call(
        momentum_kernel,
        out_shape=jax.ShapeDtypeStruct(momentum.shape, f32),
        scratch_shapes=[pltpu.VMEM((tiles * pair, pair), f32)],
        compiler_params=kernel_room,
        cost_estimate=small,
        name="momentum_step",
    )(own_sum, rest, momentum, row_waves, col_waves)


def fold_kernel(parts_ref, _, out_ref):
    total = parts_ref[0]
    for part in range(1, parts_ref.shape[0]):
        total += parts_ref[part]
    for target in range(out_ref.shape[0]):
        out_ref[target] = total


def fold(parts, after):
    return pl.pallas_call(
        fold_kernel,
        out_shape=jax.ShapeDtypeStruct((4,) + parts.shape[1:], f32),
        in_specs=[in_vmem, pl.BlockSpec(memory_space=pl.ANY)],
        cost_estimate=small,
        name="fold",
    )(parts, after)


def weight_rows(parts_ref, line):
    parts = [parts_ref[part, line].astype(f32) for part in range(parts_ref.shape[0])]
    eighth = parts[0].shape[0] // 2
    return jnp.concatenate([p[:eighth] for p in parts] + [p[eighth:] for p in parts], axis=0)


def weight_kernel(nodes, table_ref, spots_ref, total_ref, parts_ref, out_ref):
    lines = spots_ref.shape[0]
    total = total_ref[0]
    for part in range(1, total_ref.shape[0]):
        total += total_ref[part]
    total = total / nodes
    each = total.shape[0] // lines
    table = table_ref[...]
    for line in range(lines):
        weight = weight_rows(parts_ref, line)
        row_high, row_low, col_waves = waves(table, line_spots(spots_ref, line, each))
        mean = jnp.concatenate([total[line * each + tile : line * each + tile + 1] for tile in range(each)], axis=1)
        high, low = split2(mean * col_waves)
        for tile in range(each):
            q = line * each + tile
            at = slice(tile * pair, (tile + 1) * pair)
            field = dot(
                jnp.concatenate([row_high[:, at], row_low[:, at]], axis=1),
                jnp.concatenate([high[:, at], high[:, at]], axis=1),
                ((1,), (1,)),
            )
            field += dot(row_high[:, at], low[:, at], ((1,), (1,)))
            fresh = weight[at] - learn_rate * jnp.tanh(field)
            out_ref[q * pair : (q + 1) * pair, :] = fresh.astype(bf16)


def new_weight_of(table, spots, total, parts, nodes):
    return pl.pallas_call(
        functools.partial(weight_kernel, nodes),
        out_shape=jax.ShapeDtypeStruct((total.shape[1] * pair, pair), bf16),
        compiler_params=kernel_room,
        cost_estimate=small,
        name="weight_step",
    )(table, spots, total, parts)


def input_kernel(hidden_ref, gain_ref, cot_ref, parts_ref, out_ref, gained_ref):
    features = hidden_ref.shape[1]
    wide = hidden_ref[...].astype(f32)
    scale = lax.rsqrt(jnp.sum(wide * wide, axis=1, keepdims=True) * (1.0 / features) + epsilon)
    cot = cot_ref[...]
    lines = parts_ref.shape[1]
    step = features // lines
    along = jnp.zeros(scale.shape, f32)
    for piece in range(lines):
        at = slice(piece * step, (piece + 1) * step)
        weight = weight_rows(parts_ref, piece).astype(bf16)
        gained = gain_ref[:, at] * dot(cot, weight, ((1,), (1,)))
        gained_ref[:, at] = gained
        along += jnp.sum(hidden_ref[:, at].astype(f32) * gained, axis=1, keepdims=True)
    factor = scale**3 * (along * (1.0 / features))
    for piece in range(lines):
        at = slice(piece * step, (piece + 1) * step)
        out_ref[:, at] = (scale * gained_ref[:, at] - hidden_ref[:, at].astype(f32) * factor).astype(bf16)


def input_grad_of(hidden, gain, cot, parts):
    return pl.pallas_call(
        input_kernel,
        out_shape=jax.ShapeDtypeStruct(hidden.shape, bf16),
        scratch_shapes=[pltpu.VMEM(hidden.shape, f32)],
        compiler_params=kernel_room,
        cost_estimate=small,
        name="input_gradient",
    )(hidden, gain, cot, parts)


def on_device(hidden, gain, cotangent, weight, momentum, indices):
    nodes, owners = lax.axis_size("node"), lax.axis_size("local")
    node, local = lax.axis_index("node"), lax.axis_index("local")
    features = hidden.shape[1]
    own_rows, head = weight.shape
    table = wave_table()
    blocks = indices.size
    row_of, col_of = indices // side, indices % side

    upper = local % 2
    eighth = own_rows // 8
    part = (node // 8) * 2 + node % 2
    with jax.named_scope("weight_part"):
        piece = lax.dynamic_slice_in_dim(weight, part * eighth, eighth, axis=0)
        at_half = lambda spots: lax.dynamic_update_slice(
            jnp.zeros((8 * pair,), jnp.int32), spots.reshape(-1), (upper * blocks,)
        ).reshape(8, pair)
        piece = jnp.concatenate([piece, at_half(row_of).astype(bf16), at_half(col_of).astype(bf16)], axis=0)
    with jax.named_scope("weight_over_y"):
        other = hop(piece, lambda x, y, z, c: (x, (y + (2 if y in (2, 3, 6, 7) else 6)) % 8, z, c))

    spare = (-blocks) % pair
    tiles = (blocks + spare) // pair
    own_spots = jnp.stack([row_of.reshape(-1), col_of.reshape(-1)])
    own_spots = jnp.pad(own_spots, ((0, 0), (0, spare))).reshape(2 * tiles, pair)
    own_momentum = momentum[0]
    row_waves, col_waves, decayed = own_waves(table, own_spots, own_momentum)
    decayed = lax.dynamic_update_slice(
        jnp.zeros((owners * blocks,), f32), decayed.reshape(-1)[:blocks], (local * blocks,)
    ).reshape(-1, pair)

    with jax.named_scope("weight_over_z"):
        gathered = over_z(pack(upper, piece, other, decayed))

    message, high, low = front(hidden, gain[None, :], cotangent, owners)
    with jax.named_scope("gradient_exchange"):
        arrived = over_z(message)

    total = pick(table, gathered, high, low, decayed)
    with jax.named_scope("coefficients"):
        total = total + hop(total, lambda x, y, z, c: (x, y, z, 1 - c))
        total = total + hop(total, lambda x, y, z, c: (x, y ^ 1, z, c))
        total = total + hop(total, lambda x, y, z, c: (x, ((y + 1) ^ 1) - 1, z, c))
        total = total + hop(total, lambda x, y, z, c: (x, y ^ 3 if y in (0, 3, 4, 7) else 7 - y, z, c))
    own_sum, rest, spread = middle(arrived, upper, total)
    with jax.named_scope("coefficients_over_z"):
        totals = over_z(spread)
    with jax.named_scope("gradient_over_y"):
        rest = hop(rest, lambda x, y, z, c: (x, (y + 4) % 8, z, c))

    with jax.named_scope("weight_over_x_and_core"):
        parts = lax.all_gather(gathered[:, : 2 * eighth, :], "node", axis_index_groups=x_core_groups)

    input_grad = input_grad_of(hidden, gain[None, :], cotangent, parts)
    with jax.named_scope("coefficients_over_x"):
        totals = lax.all_to_all(fold(totals, input_grad), "node", 0, 0, axis_index_groups=x_groups)
    new_momentum = new_momentum_of(own_sum, rest, own_momentum, row_waves, col_waves)[None]
    new_weight = new_weight_of(table, gathered, totals, parts, nodes)
    return (new_weight, new_momentum, input_grad)


def solution(mesh):
    return jax.shard_map(
        on_device,
        mesh=mesh,
        in_specs=(
            P(("node", "local"), None),
            P(),
            P(("node", "local"), None),
            P("local", None),
            P("node", "local", None),
            P("local", None),
        ),
        out_specs=(P(), P("node", "local", None), P(("node", "local"), None)),
        check_vma=False,
    )
```

```python
import functools

import jax
import jax.numpy as jnp
from jax import lax
from jax.experimental import pallas as pl
from jax.experimental.pallas import tpu as pltpu
from jax.sharding import PartitionSpec as P

epsilon = 1e-06
decay_rate = 0.9
learn_rate = 0.01
side = 64
pair = 128
f32 = jnp.float32
bf16 = jnp.bfloat16
kernel_room = pltpu.CompilerParams(vmem_limit_bytes=12 * 2**20)
small = pl.CostEstimate(flops=1, bytes_accessed=1, transcendentals=0)

z_groups = [[2 * z + h for z in range(8)] for h in range(2)]
x_core_groups = [[8 * x + 2 * r + c for x in range(4) for c in range(2)] for r in range(4)]


def whole_mesh(move):
    def index(x, y, z, core):
        return ((x * 4 + y % 4) * 2 + core) * 16 + z * 2 + y // 4

    places = [(x, y, z, c) for x in range(4) for y in range(8) for z in range(8) for c in range(2)]
    sizes = (4, 8, 8, 2)
    wrap = lambda place: [at % size for at, size in zip(place, sizes)]
    return [(index(*place), index(*wrap(move(*place)))) for place in places]


def hop(value, move):
    return lax.ppermute(value, ("node", "local"), whole_mesh(move))


def over_z(value):
    return lax.all_to_all(value, "local", 0, 0, axis_index_groups=z_groups)


def dct_table():
    freq = jnp.arange(side, dtype=f32)[:, None]
    place = jnp.arange(side, dtype=f32)[None, :]
    wave = jnp.cos(jnp.pi * (2.0 * place + 1.0) * freq / (2.0 * side))
    norm_row = jnp.where(freq == 0.0, jnp.sqrt(1.0 / side), jnp.sqrt(2.0 / side))
    return wave * norm_row


def split2(value):
    high = value.astype(bf16)
    return high, (value - high.astype(f32)).astype(bf16)


def wave_table():
    turned = dct_table().T
    high = lax.reduce_precision(turned, exponent_bits=8, mantissa_bits=7)
    low = turned - high
    empty = jnp.zeros_like(turned)
    return jnp.block([[high, empty], [low, empty], [empty, high], [empty, low]]).astype(bf16)


def dot(a, b, dims):
    return lax.dot_general(a, b, (dims, ((), ())), preferred_element_type=f32)


def from_hbm(value):
    return pltpu.with_memory_space_constraint(value, pltpu.HBM)


in_hbm = pl.BlockSpec(memory_space=pltpu.HBM)
in_vmem = pl.BlockSpec(memory_space=pltpu.VMEM)
in_smem = pl.BlockSpec(memory_space=pltpu.SMEM)


def waves(table, spots):
    tiles = spots.shape[0] // 2
    rows = jnp.concatenate([spots[at : at + 1] for at in range(tiles)], axis=1)
    cols = jnp.concatenate([spots[at : at + 1] for at in range(tiles, 2 * tiles)], axis=1)
    wide = (side, tiles * pair)
    at = lax.broadcasted_iota(jnp.int32, wide, 0)
    chosen = jnp.concatenate([jnp.where(at == rows, 1.0, 0.0), jnp.where(at == cols, 1.0, 0.0)], axis=0)
    found = dot(table, chosen.astype(bf16), ((1,), (0,)))
    block = lax.broadcasted_iota(jnp.int32, wide, 1) // 32 % 4

    def placed(value, second):
        return jnp.concatenate([jnp.where(second, 0.0, value), jnp.where(second, value, 0.0)], axis=0)

    below, right = block >= 2, block % 2 == 1
    row_high = placed(found[:side], below).astype(bf16)
    row_low = placed(found[side : 2 * side], below).astype(bf16)
    return row_high, row_low, placed(found[2 * side : 3 * side] + found[3 * side :], right)


def coded(value):
    top = jnp.max(jnp.abs(value), axis=0, keepdims=True)
    power = jnp.clip(jnp.ceil(jnp.log2(top * (1.0 / 32000.0))), -120.0, 120.0)
    whole = jnp.round(value * jnp.exp2(-power)).astype(jnp.int32).astype(jnp.int16)
    return whole, jnp.broadcast_to(power.astype(jnp.int32), (16, pair)).astype(jnp.int16)


def decoded(whole, power):
    return whole.astype(jnp.int32).astype(f32) * jnp.exp2(power.astype(jnp.int32)[0:1, :].astype(f32))


def picked_from(tile, row_high, row_low, col_waves):
    high, low = split2(tile)
    half = dot(jnp.concatenate([high, low], axis=0), jnp.concatenate([row_high, row_high], axis=0), ((0,), (0,)))
    half += dot(high, row_low, ((0,), (0,)))
    return jnp.sum(half * col_waves, axis=0, keepdims=True)


def field_from(picked, row_high, row_low, col_waves):
    high, low = split2(picked * col_waves)
    field = dot(jnp.concatenate([row_high, row_low], axis=1), jnp.concatenate([high, high], axis=1), ((1,), (1,)))
    return field + dot(row_high, low, ((1,), (1,)))


def front_kernel(
    table_ref, spots_ref, hidden_in_ref, gain_in_ref, cot_in_ref, momentum_in_ref,
    message_out_ref, high_out_ref, low_out_ref, picked_ref,
    hidden_ref, gain_ref, cot_ref, momentum_ref, message_ref, high_ref, low_ref,
    read, hidden_read, message_done, high_done, low_done,
):
    lines, _, tall, _ = message_ref.shape
    rows = tall - 16
    features = hidden_ref.shape[1]
    spans = [slice(line * 2 * rows, (line + 1) * 2 * rows) for line in range(lines)]
    reads = [
        pltpu.make_async_copy(source, target, read.at[at])
        for at, (source, target) in enumerate(
            [(momentum_in_ref, momentum_ref), (cot_in_ref, cot_ref), (gain_in_ref, gain_ref)]
        )
    ]
    hidden_reads = [
        pltpu.make_async_copy(hidden_in_ref.at[:, at], hidden_ref.at[:, at], hidden_read.at[line])
        for line, at in enumerate(spans)
    ]
    for copy in reads + hidden_reads:
        copy.start()
    own = waves(table_ref[...], spots_ref[...])
    reads[0].wait()
    for q in range(picked_ref.shape[0]):
        tile = decay_rate * momentum_ref[q * pair : min((q + 1) * pair, rows), :]
        short = pair - tile.shape[0]
        if short:
            tile = jnp.concatenate([tile, jnp.zeros((short, pair), f32)], axis=0)
        picked_ref[q : q + 1, :] = picked_from(tile, *[part[:, q * pair : (q + 1) * pair] for part in own])
    square = jnp.zeros((hidden_ref.shape[0], 1), f32)
    for line, at in enumerate(spans):
        hidden_reads[line].wait()
        wide = hidden_ref[:, at].astype(f32)
        square += jnp.sum(wide * wide, axis=1, keepdims=True)
    scale = lax.rsqrt(square * (1.0 / features) + epsilon)
    reads[1].wait()
    reads[2].wait()
    cot = cot_ref[...]
    copies = []
    for line, at in enumerate(spans):
        normed = (hidden_ref[:, at].astype(f32) * scale * gain_ref[:, at]).astype(bf16)
        term = dot(normed, cot, ((0,), (0,)))
        for half in range(2):
            own = term[half * rows : (half + 1) * rows]
            message_ref[line, half, 0:rows, :], message_ref[line, half, rows:tall, :] = coded(own)
        high_ref[line], low_ref[line] = split2(dot(cot, normed, ((0,), (0,))))
        for source, target, done in (
            (message_ref, message_out_ref, message_done),
            (high_ref, high_out_ref, high_done),
            (low_ref, low_out_ref, low_done),
        ):
            copies.append(pltpu.make_async_copy(source.at[line], target.at[line], done.at[line]))
            copies[-1].start()
    for copy in copies:
        copy.wait()


def front(table, spots, hidden, gain, cot, momentum, owners):
    tokens, features = hidden.shape
    lines, rows = owners // 2, features // owners
    ins = (hidden, gain, cot, momentum)
    outs = (
        pltpu.HBM((lines, 2, rows + 16, pair), jnp.int16),
        pltpu.HBM((lines, pair, 2 * rows), bf16),
        pltpu.HBM((lines, pair, 2 * rows), bf16),
    )
    return pl.pallas_call(
        front_kernel,
        out_shape=outs + (jax.ShapeDtypeStruct((spots.shape[0] // 2, pair), f32),),
        in_specs=[in_vmem, in_vmem] + [in_hbm] * 4,
        out_specs=(in_hbm,) * 3 + (in_vmem,),
        scratch_shapes=[pltpu.VMEM(value.shape, value.dtype) for value in ins + outs]
        + [pltpu.SemaphoreType.DMA((count,)) for count in (3, lines, lines, lines, lines)],
        compiler_params=kernel_room,
        cost_estimate=small,
        name="front",
    )(table, spots, *[from_hbm(value) for value in ins])


def line_spots(spots_ref, line, tiles):
    tall = spots_ref.shape[1]
    spots = spots_ref[line, tall - 16 : tall, :].astype(f32).astype(jnp.int32)
    return jnp.concatenate([spots[:tiles], spots[8 : 8 + tiles]], axis=0)


def pick_kernel(
    table_ref, spots_ref, high_in_ref, low_in_ref, decayed_ref, picked_ref, high_ref, low_ref, high_done, low_done
):
    lines = spots_ref.shape[0]
    tiles = picked_ref.shape[0]
    each = tiles // lines
    arrivals = []
    for line in range(lines):
        arrivals.append(pltpu.make_async_copy(high_in_ref.at[line], high_ref.at[line], high_done.at[line]))
        arrivals.append(pltpu.make_async_copy(low_in_ref.at[line], low_ref.at[line], low_done.at[line]))
        arrivals[-2].start()
        arrivals[-1].start()
    table = table_ref[...]
    for line in range(lines):
        row_high, row_low, col_waves = waves(table, line_spots(spots_ref, line, each))
        arrivals[2 * line].wait()
        arrivals[2 * line + 1].wait()
        for tile in range(each):
            q = line * each + tile
            at = slice(tile * pair, (tile + 1) * pair)
            high = high_ref[line, :, at]
            both = jnp.concatenate([high, low_ref[line, :, at]], axis=1)
            half = dot(both, jnp.concatenate([row_high[:, at], row_high[:, at]], axis=0), ((1,), (0,)))
            half += dot(high, row_low[:, at], ((1,), (0,)))
            picked_ref[q : q + 1, :] = decayed_ref[q : q + 1, :] + jnp.sum(
                half * col_waves[:, at], axis=0, keepdims=True
            )


def pick(table, spots, high, low, decayed):
    lines = spots.shape[0]
    return pl.pallas_call(
        pick_kernel,
        out_shape=jax.ShapeDtypeStruct(decayed.shape, f32),
        in_specs=[in_vmem, in_vmem, in_hbm, in_hbm, in_vmem],
        scratch_shapes=[pltpu.VMEM(high.shape, bf16)] * 2 + [pltpu.SemaphoreType.DMA((lines,))] * 2,
        compiler_params=kernel_room,
        cost_estimate=small,
        name="pick",
    )(table, spots, from_hbm(high), from_hbm(low), decayed)


def middle_kernel(upper_ref, message_ref, total_ref, own_ref, rest_out_ref, spread_ref, rest_ref, rest_done):
    sources, halves, tall, _ = message_ref.shape
    rows = own_ref.shape[0]
    sums = []
    for half in range(halves):
        term = jnp.zeros(own_ref.shape, f32)
        for source in range(sources):
            term += decoded(message_ref[source, half, 0:rows, :], message_ref[source, half, rows:tall, :])
        sums.append(term)
    first = upper_ref[0] == 0
    own_ref[...] = jnp.where(first, sums[0], sums[1])
    rest_ref[0:rows, :], rest_ref[rows:tall, :] = coded(jnp.where(first, sums[1], sums[0]))
    copy = pltpu.make_async_copy(rest_ref, rest_out_ref, rest_done)
    copy.start()
    for source in range(sources):
        spread_ref[source] = total_ref[...]
    copy.wait()


def middle(message, upper, total):
    sources, _, tall, _ = message.shape
    return pl.pallas_call(
        middle_kernel,
        out_shape=(
            jax.ShapeDtypeStruct((tall - 16, pair), f32),
            pltpu.HBM((tall, pair), jnp.int16),
            jax.ShapeDtypeStruct((sources,) + total.shape, f32),
        ),
        out_specs=(in_vmem, in_hbm, in_vmem),
        scratch_shapes=[pltpu.VMEM((tall, pair), jnp.int16), pltpu.SemaphoreType.DMA],
        in_specs=[in_smem, in_vmem, in_vmem],
        compiler_params=kernel_room,
        cost_estimate=small,
        name="middle",
    )(upper[None], message, total)


def momentum_kernel(table_ref, spots_ref, sum_ref, rest_ref, momentum_ref, out_ref, mid_ref):
    rows = out_ref.shape[0]
    row_high, row_low, col_waves = waves(table_ref[...], spots_ref[...])
    total = decay_rate * momentum_ref[...] + sum_ref[...]
    mid_ref[0:rows, :] = total + decoded(rest_ref[0:rows, :], rest_ref[rows:, :])
    mid_ref[rows:, :] = jnp.zeros((mid_ref.shape[0] - rows, pair), f32)
    for q in range(mid_ref.shape[0] // pair):
        at = slice(q * pair, (q + 1) * pair)
        own = row_high[:, at], row_low[:, at], col_waves[:, at]
        tile = mid_ref[at, :]
        sent = field_from(picked_from(tile, *own), *own)
        left = min(pair, rows - q * pair)
        out_ref[q * pair : q * pair + left, :] = (tile - sent)[:left]


def new_momentum_of(table, spots, own_sum, rest, momentum):
    return pl.pallas_call(
        momentum_kernel,
        out_shape=jax.ShapeDtypeStruct(momentum.shape, f32),
        scratch_shapes=[pltpu.VMEM((spots.shape[0] // 2 * pair, pair), f32)],
        compiler_params=kernel_room,
        cost_estimate=small,
        name="momentum_step",
    )(table, spots, own_sum, rest, momentum)


def fold_kernel(parts_ref, _, __, out_ref):
    total = parts_ref[0]
    for part in range(1, parts_ref.shape[0]):
        total += parts_ref[part]
    for target in range(out_ref.shape[0]):
        out_ref[target] = total


def fold(parts, *after):
    return pl.pallas_call(
        fold_kernel,
        out_shape=jax.ShapeDtypeStruct((8,) + parts.shape[1:], f32),
        in_specs=[in_vmem, in_hbm, in_hbm],
        compiler_params=kernel_room,
        cost_estimate=small,
        name="fold",
    )(parts, *[from_hbm(value) for value in after])


def weight_rows(parts_ref, line):
    parts = [parts_ref[part, line].astype(f32) for part in range(parts_ref.shape[0])]
    eighth = parts[0].shape[0] // 2
    return jnp.concatenate([p[:eighth] for p in parts] + [p[eighth:] for p in parts], axis=0)


def weight_kernel(nodes, table_ref, spots_ref, total_ref, parts_ref, out_ref):
    lines = spots_ref.shape[0]
    total = total_ref[0]
    for part in range(1, total_ref.shape[0]):
        total += total_ref[part]
    total = total / nodes
    each = total.shape[0] // lines
    table = table_ref[...]
    for line in range(lines):
        weight = weight_rows(parts_ref, line)
        row_high, row_low, col_waves = waves(table, line_spots(spots_ref, line, each))
        mean = jnp.concatenate([total[line * each + tile : line * each + tile + 1] for tile in range(each)], axis=1)
        for tile in range(each):
            q = line * each + tile
            at = slice(tile * pair, (tile + 1) * pair)
            field = field_from(mean[:, at], row_high[:, at], row_low[:, at], col_waves[:, at])
            fresh = weight[at] - learn_rate * jnp.tanh(field)
            out_ref[q * pair : (q + 1) * pair, :] = fresh.astype(bf16)


def new_weight_of(table, spots, total, parts, nodes):
    return pl.pallas_call(
        functools.partial(weight_kernel, nodes),
        out_shape=jax.ShapeDtypeStruct((total.shape[1] * pair, pair), bf16),
        compiler_params=kernel_room,
        cost_estimate=small,
        name="weight_step",
    )(table, spots, total, parts)


def input_kernel(
    hidden_ref, gain_in_ref, cot_in_ref, parts_in_ref, out_ref, gain_ref, cot_ref, parts_ref, gained_ref, read
):
    lines = parts_ref.shape[1]
    features = hidden_ref.shape[1]
    step = features // lines
    spans = [slice(line * step, (line + 1) * step) for line in range(lines)]
    reads = [
        pltpu.make_async_copy(source, target, read.at[at])
        for at, (source, target) in enumerate(
            [(parts_in_ref, parts_ref), (cot_in_ref, cot_ref), (gain_in_ref, gain_ref)]
        )
    ]
    for copy in reads:
        copy.start()
    square = jnp.zeros((hidden_ref.shape[0], 1), f32)
    for at in spans:
        wide = hidden_ref[:, at].astype(f32)
        square += jnp.sum(wide * wide, axis=1, keepdims=True)
    scale = lax.rsqrt(square * (1.0 / features) + epsilon)
    for copy in reads:
        copy.wait()
    cot = cot_ref[...]
    along = jnp.zeros(scale.shape, f32)
    for line, at in enumerate(spans):
        weight = weight_rows(parts_ref, line).astype(bf16)
        gained = gain_ref[:, at] * dot(cot, weight, ((1,), (1,)))
        gained_ref[:, at] = gained
        along += jnp.sum(hidden_ref[:, at].astype(f32) * gained, axis=1, keepdims=True)
    factor = scale**3 * (along * (1.0 / features))
    for at in spans:
        out_ref[:, at] = (scale * gained_ref[:, at] - hidden_ref[:, at].astype(f32) * factor).astype(bf16)


def input_grad_of(hidden, gain, cot, parts):
    ins = (gain, cot, parts)
    return pl.pallas_call(
        input_kernel,
        out_shape=jax.ShapeDtypeStruct(hidden.shape, bf16),
        in_specs=[in_vmem] + [in_hbm] * 3,
        scratch_shapes=[pltpu.VMEM(value.shape, value.dtype) for value in ins]
        + [pltpu.VMEM(hidden.shape, f32), pltpu.SemaphoreType.DMA((3,))],
        compiler_params=kernel_room,
        cost_estimate=small,
        name="input_gradient",
    )(hidden, *[from_hbm(value) for value in ins])


def on_device(hidden, gain, cotangent, weight, momentum, indices):
    nodes, owners = lax.axis_size("node"), lax.axis_size("local")
    node, local = lax.axis_index("node"), lax.axis_index("local")
    features = hidden.shape[1]
    own_rows, head = weight.shape
    table = wave_table()
    blocks = indices.size
    row_of, col_of = indices >> 6, indices & (side - 1)

    upper = local % 2
    eighth = own_rows // 8
    part = (node // 8) * 2 + node % 2
    with jax.named_scope("weight_part"):
        piece = lax.dynamic_slice_in_dim(weight, part * eighth, eighth, axis=0)
        at_half = lambda spots: lax.dynamic_update_slice(
            jnp.zeros((8 * pair,), jnp.int32), spots.reshape(-1), (upper * blocks,)
        ).reshape(8, pair)
        piece = jnp.concatenate([piece, at_half(row_of).astype(bf16), at_half(col_of).astype(bf16)], axis=0)
    with jax.named_scope("weight_over_z"):
        gathered = over_z(jnp.broadcast_to(piece[None], (8,) + piece.shape))

    spare = (-blocks) % pair
    tiles = (blocks + spare) // pair
    own_spots = jnp.stack([row_of.reshape(-1), col_of.reshape(-1)])
    own_spots = jnp.pad(own_spots, ((0, 0), (0, spare))).reshape(2 * tiles, pair)
    own_momentum = momentum[0]
    message, high, low, decayed = front(
        table, own_spots, hidden, gain[None, :], cotangent, own_momentum, owners
    )
    decayed = lax.dynamic_update_slice(
        jnp.zeros((owners * blocks,), f32), decayed.reshape(-1)[:blocks], (local * blocks,)
    ).reshape(-1, pair)

    with jax.named_scope("gradient_exchange"):
        arrived = over_z(message)

    with jax.named_scope("weight_over_y"):
        other = hop(gathered, lambda x, y, z, c: (x, (y + (2 if y in (2, 3, 6, 7) else 6)) % 8, z, c))
        spots = gathered[:, eighth:] + other[:, eighth:]
        mine, other = gathered[:, None, :eighth], other[:, None, :eighth]
        pieces = jnp.where(upper == 0, jnp.concatenate([mine, other], 1), jnp.concatenate([other, mine], 1))
        pieces = pieces.reshape(8, 2 * eighth, head)

    total = pick(table, spots, high, low, decayed)
    with jax.named_scope("coefficients"):
        total = total + hop(total, lambda x, y, z, c: (x, y ^ 1, z, c))
        total = total + hop(total, lambda x, y, z, c: (x, ((y + 1) ^ 1) - 1, z, c))
        total = total + hop(total, lambda x, y, z, c: (x, y ^ 3 if y in (0, 3, 4, 7) else 7 - y, z, c))
    own_sum, rest, spread = middle(arrived, upper, total)
    with jax.named_scope("coefficients_over_z"):
        totals = over_z(spread)
    with jax.named_scope("gradient_over_y"):
        rest = hop(rest, lambda x, y, z, c: (x, (y + 4) % 8, z, c))

    with jax.named_scope("weight_over_x_and_core"):
        parts = lax.all_gather(pieces, "node", axis_index_groups=x_core_groups)

    input_grad = input_grad_of(hidden, gain[None, :], cotangent, parts)
    with jax.named_scope("coefficients_over_x_and_core"):
        totals = lax.all_to_all(fold(totals, rest, input_grad), "node", 0, 0, axis_index_groups=x_core_groups)
    new_momentum = new_momentum_of(table, own_spots, own_sum, rest, own_momentum)[None]
    new_weight = new_weight_of(table, spots, totals, parts, nodes)
    return (new_weight, new_momentum, input_grad)


def solution(mesh):
    return jax.shard_map(
        on_device,
        mesh=mesh,
        in_specs=(
            P(("node", "local"), None),
            P(),
            P(("node", "local"), None),
            P("local", None),
            P("node", "local", None),
            P("local", None),
        ),
        out_specs=(P(), P("node", "local", None), P(("node", "local"), None)),
        check_vma=False,
    )
```

```python
import functools

import jax
import jax.numpy as jnp
from jax import lax
from jax.experimental import pallas as pl
from jax.experimental.pallas import tpu as pltpu
from jax.sharding import PartitionSpec as P

epsilon = 1e-06
decay_rate = 0.9
learn_rate = 0.01
side = 64
pair = 128
f32 = jnp.float32
bf16 = jnp.bfloat16
kernel_room = pltpu.CompilerParams(vmem_limit_bytes=12 * 2**20)
small = pl.CostEstimate(flops=1, bytes_accessed=1, transcendentals=0)

z_groups = [[2 * z + h for z in range(8)] for h in range(2)]
core_groups = [[2 * i, 2 * i + 1] for i in range(16)]
x_core_groups = [[8 * x + 2 * r + c for x in range(4) for c in range(2)] for r in range(4)]


def whole_mesh(move):
    def index(x, y, z, core):
        return ((x * 4 + y % 4) * 2 + core) * 16 + z * 2 + y // 4

    places = [(x, y, z, c) for x in range(4) for y in range(8) for z in range(8) for c in range(2)]
    sizes = (4, 8, 8, 2)
    wrap = lambda place: [at % size for at, size in zip(place, sizes)]
    return [(index(*place), index(*wrap(move(*place)))) for place in places]


def hop(value, move):
    return lax.ppermute(value, ("node", "local"), whole_mesh(move))


def over_z(value):
    return lax.all_to_all(value, "local", 0, 0, axis_index_groups=z_groups)


def dct_table():
    freq = jnp.arange(side, dtype=f32)[:, None]
    place = jnp.arange(side, dtype=f32)[None, :]
    wave = jnp.cos(jnp.pi * (2.0 * place + 1.0) * freq / (2.0 * side))
    norm_row = jnp.where(freq == 0.0, jnp.sqrt(1.0 / side), jnp.sqrt(2.0 / side))
    return wave * norm_row


def split2(value):
    high = value.astype(bf16)
    return high, (value - high.astype(f32)).astype(bf16)


def wave_table():
    turned = dct_table().T
    high = lax.reduce_precision(turned, exponent_bits=8, mantissa_bits=7)
    low = turned - high
    empty = jnp.zeros_like(turned)
    return jnp.block([[high, empty], [low, empty], [empty, high], [empty, low]]).astype(bf16)


def dot(a, b, dims):
    return lax.dot_general(a, b, (dims, ((), ())), preferred_element_type=f32)


def from_hbm(value):
    return pltpu.with_memory_space_constraint(value, pltpu.HBM)


in_hbm = pl.BlockSpec(memory_space=pltpu.HBM)
in_vmem = pl.BlockSpec(memory_space=pltpu.VMEM)
in_smem = pl.BlockSpec(memory_space=pltpu.SMEM)


def waves(table, spots):
    tiles = spots.shape[0] // 2
    rows = jnp.concatenate([spots[at : at + 1] for at in range(tiles)], axis=1)
    cols = jnp.concatenate([spots[at : at + 1] for at in range(tiles, 2 * tiles)], axis=1)
    wide = (side, tiles * pair)
    at = lax.broadcasted_iota(jnp.int32, wide, 0)
    chosen = jnp.concatenate([jnp.where(at == rows, 1.0, 0.0), jnp.where(at == cols, 1.0, 0.0)], axis=0)
    found = dot(table, chosen.astype(bf16), ((1,), (0,)))
    block = lax.broadcasted_iota(jnp.int32, wide, 1) // 32 % 4

    def placed(value, second):
        return jnp.concatenate([jnp.where(second, 0.0, value), jnp.where(second, value, 0.0)], axis=0)

    below, right = block >= 2, block % 2 == 1
    row_high = placed(found[:side], below).astype(bf16)
    row_low = placed(found[side : 2 * side], below).astype(bf16)
    return row_high, row_low, placed(found[2 * side : 3 * side] + found[3 * side :], right)


def coded(value):
    top = jnp.max(jnp.abs(value), axis=0, keepdims=True)
    power = jnp.clip(jnp.ceil(jnp.log2(top * (1.0 / 32000.0))), -120.0, 120.0)
    whole = jnp.round(value * jnp.exp2(-power)).astype(jnp.int32)
    place = lax.broadcasted_iota(jnp.int32, (8, pair), 0)
    bits = ((power.astype(jnp.int32) + 128) >> place) & 1
    return jnp.concatenate([(whole[:8] & -2) | bits, whole[8:]], axis=0).astype(jnp.int16)


def decoded(message):
    whole = message.astype(jnp.int32)
    place = lax.broadcasted_iota(jnp.int32, (8, pair), 0)
    power = jnp.sum(((whole[:8] & 1) << place).astype(f32), axis=0, keepdims=True) - 128.0
    return whole.astype(f32) * jnp.exp2(power)


def picked_from(tile, row_high, row_low, col_waves):
    high, low = split2(tile)
    half = dot(jnp.concatenate([high, low], axis=0), jnp.concatenate([row_high, row_high], axis=0), ((0,), (0,)))
    half += dot(high, row_low, ((0,), (0,)))
    return jnp.sum(half * col_waves, axis=0, keepdims=True)


def field_from(picked, row_high, row_low, col_waves):
    high, low = split2(picked * col_waves)
    field = dot(jnp.concatenate([row_high, row_low], axis=1), jnp.concatenate([high, high], axis=1), ((1,), (1,)))
    return field + dot(row_high, low, ((1,), (1,)))


def front_kernel(
    table_ref, spots_ref, hidden_in_ref, gain_in_ref, cot_in_ref, momentum_in_ref,
    message_out_ref, high_out_ref, low_out_ref, picked_ref,
    hidden_ref, gain_ref, cot_ref, momentum_ref, message_ref, high_ref, low_ref,
    read, hidden_read, message_done, high_done, low_done,
):
    lines, _, rows, _ = message_ref.shape
    features = hidden_ref.shape[1]
    spans = [slice(line * 2 * rows, (line + 1) * 2 * rows) for line in range(lines)]
    reads = [
        pltpu.make_async_copy(source, target, read.at[at])
        for at, (source, target) in enumerate(
            [(momentum_in_ref, momentum_ref), (cot_in_ref, cot_ref), (gain_in_ref, gain_ref)]
        )
    ]
    hidden_reads = [
        pltpu.make_async_copy(hidden_in_ref.at[:, at], hidden_ref.at[:, at], hidden_read.at[line])
        for line, at in enumerate(spans)
    ]
    for copy in reads + hidden_reads:
        copy.start()
    own = waves(table_ref[...], spots_ref[...])
    reads[0].wait()
    for q in range(picked_ref.shape[0]):
        tile = decay_rate * momentum_ref[q * pair : min((q + 1) * pair, rows), :]
        short = pair - tile.shape[0]
        if short:
            tile = jnp.concatenate([tile, jnp.zeros((short, pair), f32)], axis=0)
        picked_ref[q : q + 1, :] = picked_from(tile, *[part[:, q * pair : (q + 1) * pair] for part in own])
    square = jnp.zeros((hidden_ref.shape[0], 1), f32)
    for line, at in enumerate(spans):
        hidden_reads[line].wait()
        wide = hidden_ref[:, at].astype(f32)
        square += jnp.sum(wide * wide, axis=1, keepdims=True)
    scale = lax.rsqrt(square * (1.0 / features) + epsilon)
    reads[1].wait()
    reads[2].wait()
    cot = cot_ref[...]
    copies = []
    for line, at in enumerate(spans):
        normed = (hidden_ref[:, at].astype(f32) * scale * gain_ref[:, at]).astype(bf16)
        term = dot(normed, cot, ((0,), (0,)))
        for half in range(2):
            own = term[half * rows : (half + 1) * rows]
            message_ref[line, half] = coded(own)
        high_ref[line], low_ref[line] = split2(dot(cot, normed, ((0,), (0,))))
        for source, target, done in (
            (message_ref, message_out_ref, message_done),
            (high_ref, high_out_ref, high_done),
            (low_ref, low_out_ref, low_done),
        ):
            copies.append(pltpu.make_async_copy(source.at[line], target.at[line], done.at[line]))
            copies[-1].start()
    for copy in copies:
        copy.wait()


def front(table, spots, hidden, gain, cot, momentum, owners):
    tokens, features = hidden.shape
    lines, rows = owners // 2, features // owners
    ins = (hidden, gain, cot, momentum)
    outs = (
        pltpu.HBM((lines, 2, rows, pair), jnp.int16),
        pltpu.HBM((lines, pair, 2 * rows), bf16),
        pltpu.HBM((lines, pair, 2 * rows), bf16),
    )
    return pl.pallas_call(
        front_kernel,
        out_shape=outs + (jax.ShapeDtypeStruct((spots.shape[0] // 2, pair), f32),),
        in_specs=[in_vmem, in_vmem] + [in_hbm] * 4,
        out_specs=(in_hbm,) * 3 + (in_vmem,),
        scratch_shapes=[pltpu.VMEM(value.shape, value.dtype) for value in ins + outs]
        + [pltpu.SemaphoreType.DMA((count,)) for count in (3, lines, lines, lines, lines)],
        compiler_params=kernel_room,
        cost_estimate=small,
        name="front",
    )(table, spots, *[from_hbm(value) for value in ins])


def pack_kernel(upper_ref, mine_ref, other_ref, out_ref):
    eighth = mine_ref.shape[0] - 16
    mine, other = mine_ref[...].astype(f32), other_ref[...].astype(f32)
    first = upper_ref[0] == 0
    low = jnp.where(first, mine[:eighth], other[:eighth])
    high = jnp.where(first, other[:eighth], mine[:eighth])
    packed = jnp.concatenate([low, high, mine[eighth:] + other[eighth:]], axis=0).astype(bf16)
    for target in range(out_ref.shape[0]):
        out_ref[target] = packed


def pack(upper, mine, other):
    return pl.pallas_call(
        pack_kernel,
        out_shape=jax.ShapeDtypeStruct((8, 2 * mine.shape[0] - 16, pair), bf16),
        in_specs=[in_smem, in_vmem, in_vmem],
        compiler_params=kernel_room,
        cost_estimate=small,
        name="pack",
    )(upper[None], mine, other)


def line_spots(spots_ref, line, tiles):
    tall = spots_ref.shape[1]
    spots = spots_ref[line, tall - 16 : tall, :].astype(f32).astype(jnp.int32)
    return jnp.concatenate([spots[:tiles], spots[8 : 8 + tiles]], axis=0)


def pick_kernel(
    table_ref, spots_ref, high_in_ref, low_in_ref, decayed_ref, picked_ref, high_ref, low_ref, high_done, low_done
):
    lines = spots_ref.shape[0]
    tiles = picked_ref.shape[0]
    each = tiles // lines
    arrivals = []
    for line in range(lines):
        arrivals.append(pltpu.make_async_copy(high_in_ref.at[line], high_ref.at[line], high_done.at[line]))
        arrivals.append(pltpu.make_async_copy(low_in_ref.at[line], low_ref.at[line], low_done.at[line]))
        arrivals[-2].start()
        arrivals[-1].start()
    table = table_ref[...]
    for line in range(lines):
        row_high, row_low, col_waves = waves(table, line_spots(spots_ref, line, each))
        arrivals[2 * line].wait()
        arrivals[2 * line + 1].wait()
        for tile in range(each):
            q = line * each + tile
            at = slice(tile * pair, (tile + 1) * pair)
            high = high_ref[line, :, at]
            both = jnp.concatenate([high, low_ref[line, :, at]], axis=1)
            half = dot(both, jnp.concatenate([row_high[:, at], row_high[:, at]], axis=0), ((1,), (0,)))
            half += dot(high, row_low[:, at], ((1,), (0,)))
            picked_ref[q : q + 1, :] = decayed_ref[q : q + 1, :] + jnp.sum(
                half * col_waves[:, at], axis=0, keepdims=True
            )


def pick(table, spots, high, low, decayed):
    lines = spots.shape[0]
    return pl.pallas_call(
        pick_kernel,
        out_shape=jax.ShapeDtypeStruct(decayed.shape, f32),
        in_specs=[in_vmem, in_vmem, in_hbm, in_hbm, in_vmem],
        scratch_shapes=[pltpu.VMEM(high.shape, bf16)] * 2 + [pltpu.SemaphoreType.DMA((lines,))] * 2,
        compiler_params=kernel_room,
        cost_estimate=small,
        name="pick",
    )(table, spots, from_hbm(high), from_hbm(low), decayed)


def middle_kernel(upper_ref, message_ref, total_ref, own_ref, rest_out_ref, spread_ref, rest_ref, rest_done):
    sources, halves, _, _ = message_ref.shape
    sums = []
    for half in range(halves):
        term = jnp.zeros(own_ref.shape, f32)
        for source in range(sources):
            term += decoded(message_ref[source, half])
        sums.append(term)
    first = upper_ref[0] == 0
    own_ref[...] = jnp.where(first, sums[0], sums[1])
    rest_ref[...] = coded(jnp.where(first, sums[1], sums[0]))
    copy = pltpu.make_async_copy(rest_ref, rest_out_ref, rest_done)
    copy.start()
    for source in range(sources):
        spread_ref[source] = total_ref[...]
    copy.wait()


def middle(message, upper, total):
    sources, _, rows, _ = message.shape
    return pl.pallas_call(
        middle_kernel,
        out_shape=(
            jax.ShapeDtypeStruct((rows, pair), f32),
            pltpu.HBM((rows, pair), jnp.int16),
            jax.ShapeDtypeStruct((sources,) + total.shape, f32),
        ),
        out_specs=(in_vmem, in_hbm, in_vmem),
        scratch_shapes=[pltpu.VMEM((rows, pair), jnp.int16), pltpu.SemaphoreType.DMA],
        in_specs=[in_smem, in_vmem, in_vmem],
        compiler_params=kernel_room,
        cost_estimate=small,
        name="middle",
    )(upper[None], message, total)


def momentum_kernel(table_ref, spots_ref, sum_ref, rest_ref, momentum_ref, out_ref, mid_ref):
    rows = out_ref.shape[0]
    row_high, row_low, col_waves = waves(table_ref[...], spots_ref[...])
    total = decay_rate * momentum_ref[...] + sum_ref[...]
    mid_ref[0:rows, :] = total + decoded(rest_ref[...])
    mid_ref[rows:, :] = jnp.zeros((mid_ref.shape[0] - rows, pair), f32)
    for q in range(mid_ref.shape[0] // pair):
        at = slice(q * pair, (q + 1) * pair)
        own = row_high[:, at], row_low[:, at], col_waves[:, at]
        tile = mid_ref[at, :]
        sent = field_from(picked_from(tile, *own), *own)
        left = min(pair, rows - q * pair)
        out_ref[q * pair : q * pair + left, :] = (tile - sent)[:left]


def new_momentum_of(table, spots, own_sum, rest, momentum):
    return pl.pallas_call(
        momentum_kernel,
        out_shape=jax.ShapeDtypeStruct(momentum.shape, f32),
        scratch_shapes=[pltpu.VMEM((spots.shape[0] // 2 * pair, pair), f32)],
        compiler_params=kernel_room,
        cost_estimate=small,
        name="momentum_step",
    )(table, spots, own_sum, rest, momentum)


def fold_kernel(parts_ref, _, out_ref):
    total = parts_ref[0]
    for part in range(1, parts_ref.shape[0]):
        total += parts_ref[part]
    out_ref[...] = total


def fold(parts, after):
    return pl.pallas_call(
        fold_kernel,
        out_shape=jax.ShapeDtypeStruct(parts.shape[1:], f32),
        in_specs=[in_vmem, in_hbm],
        compiler_params=kernel_room,
        cost_estimate=small,
        name="fold",
    )(parts, from_hbm(after))


def weight_rows(parts_ref, line):
    parts = [parts_ref[part, line].astype(f32) for part in range(parts_ref.shape[0])]
    eighth = (parts[0].shape[0] - 16) // 2
    return jnp.concatenate([p[:eighth] for p in parts] + [p[eighth : 2 * eighth] for p in parts], axis=0)


def weight_kernel(nodes, table_ref, spots_ref, total_ref, other_ref, parts_ref, out_ref):
    lines = spots_ref.shape[0]
    total = (total_ref[...] + other_ref[...]) / nodes
    each = total.shape[0] // lines
    table = table_ref[...]
    for line in range(lines):
        weight = weight_rows(parts_ref, line)
        row_high, row_low, col_waves = waves(table, line_spots(spots_ref, line, each))
        mean = jnp.concatenate([total[line * each + tile : line * each + tile + 1] for tile in range(each)], axis=1)
        for tile in range(each):
            q = line * each + tile
            at = slice(tile * pair, (tile + 1) * pair)
            field = field_from(mean[:, at], row_high[:, at], row_low[:, at], col_waves[:, at])
            fresh = weight[at] - learn_rate * jnp.tanh(field)
            out_ref[q * pair : (q + 1) * pair, :] = fresh.astype(bf16)


def new_weight_of(table, spots, total, other, parts, nodes):
    return pl.pallas_call(
        functools.partial(weight_kernel, nodes),
        out_shape=jax.ShapeDtypeStruct((total.shape[0] * pair, pair), bf16),
        compiler_params=kernel_room,
        cost_estimate=small,
        name="weight_step",
    )(table, spots, total, other, parts)


def input_kernel(
    hidden_ref, gain_in_ref, cot_in_ref, parts_in_ref, out_ref, gain_ref, cot_ref, parts_ref, gained_ref, read
):
    lines = parts_ref.shape[1]
    features = hidden_ref.shape[1]
    step = features // lines
    spans = [slice(line * step, (line + 1) * step) for line in range(lines)]
    reads = [
        pltpu.make_async_copy(source, target, read.at[at])
        for at, (source, target) in enumerate(
            [(parts_in_ref, parts_ref), (cot_in_ref, cot_ref), (gain_in_ref, gain_ref)]
        )
    ]
    for copy in reads:
        copy.start()
    square = jnp.zeros((hidden_ref.shape[0], 1), f32)
    for at in spans:
        wide = hidden_ref[:, at].astype(f32)
        square += jnp.sum(wide * wide, axis=1, keepdims=True)
    scale = lax.rsqrt(square * (1.0 / features) + epsilon)
    for copy in reads:
        copy.wait()
    cot = cot_ref[...]
    along = jnp.zeros(scale.shape, f32)
    for line, at in enumerate(spans):
        weight = weight_rows(parts_ref, line).astype(bf16)
        gained = gain_ref[:, at] * dot(cot, weight, ((1,), (1,)))
        gained_ref[:, at] = gained
        along += jnp.sum(hidden_ref[:, at].astype(f32) * gained, axis=1, keepdims=True)
    factor = scale**3 * (along * (1.0 / features))
    for at in spans:
        out_ref[:, at] = (scale * gained_ref[:, at] - hidden_ref[:, at].astype(f32) * factor).astype(bf16)


def input_grad_of(hidden, gain, cot, parts):
    ins = (gain, cot, parts)
    return pl.pallas_call(
        input_kernel,
        out_shape=jax.ShapeDtypeStruct(hidden.shape, bf16),
        in_specs=[in_vmem] + [in_hbm] * 3,
        scratch_shapes=[pltpu.VMEM(value.shape, value.dtype) for value in ins]
        + [pltpu.VMEM(hidden.shape, f32), pltpu.SemaphoreType.DMA((3,))],
        compiler_params=kernel_room,
        cost_estimate=small,
        name="input_gradient",
    )(hidden, *[from_hbm(value) for value in ins])


def on_device(hidden, gain, cotangent, weight, momentum, indices):
    nodes, owners = lax.axis_size("node"), lax.axis_size("local")
    node, local = lax.axis_index("node"), lax.axis_index("local")
    features = hidden.shape[1]
    own_rows, head = weight.shape
    table = wave_table()
    blocks = indices.size
    row_of, col_of = indices >> 6, indices & (side - 1)

    upper = local % 2
    eighth = own_rows // 8
    part = (node // 8) * 2 + node % 2
    with jax.named_scope("weight_part"):
        piece = lax.dynamic_slice_in_dim(weight, part * eighth, eighth, axis=0)
        at_half = lambda spots: lax.dynamic_update_slice(
            jnp.zeros((8 * pair,), jnp.int32), spots.reshape(-1), (upper * blocks,)
        ).reshape(8, pair)
        piece = jnp.concatenate([piece, at_half(row_of).astype(bf16), at_half(col_of).astype(bf16)], axis=0)
    with jax.named_scope("weight_over_y"):
        other = hop(piece, lambda x, y, z, c: (x, (y + (2 if y in (2, 3, 6, 7) else 6)) % 8, z, c))

    spare = (-blocks) % pair
    tiles = (blocks + spare) // pair
    own_spots = jnp.stack([row_of.reshape(-1), col_of.reshape(-1)])
    own_spots = jnp.pad(own_spots, ((0, 0), (0, spare))).reshape(2 * tiles, pair)
    own_momentum = momentum[0]
    with jax.named_scope("weight_over_z"):
        gathered = over_z(pack(upper, piece, other))

    message, high, low, decayed = front(table, own_spots, hidden, gain[None, :], cotangent, own_momentum, owners)
    decayed = lax.dynamic_update_slice(
        jnp.zeros((owners * blocks,), f32), decayed.reshape(-1)[:blocks], (local * blocks,)
    ).reshape(-1, pair)
    with jax.named_scope("gradient_exchange"):
        arrived = over_z(message)

    total = pick(table, gathered, high, low, decayed)
    with jax.named_scope("coefficients"):
        total = jnp.sum(lax.all_gather(total, "node", axis_index_groups=core_groups), axis=0)
        total = total + hop(total, lambda x, y, z, c: (x, y ^ 1, z, c))
        total = total + hop(total, lambda x, y, z, c: (x, ((y + 1) ^ 1) - 1, z, c))
        total = total + hop(total, lambda x, y, z, c: (x, y ^ 3 if y in (0, 3, 4, 7) else 7 - y, z, c))
        total = total + hop(total, lambda x, y, z, c: (x ^ 1, y, z, c))
    own_sum, rest, spread = middle(arrived, upper, total)
    with jax.named_scope("coefficients_over_z"):
        totals = over_z(spread)
    with jax.named_scope("gradient_over_y"):
        rest = hop(rest, lambda x, y, z, c: (x, (y + 4) % 8, z, c))

    with jax.named_scope("weight_over_x_and_core"):
        parts = lax.all_gather(gathered, "node", axis_index_groups=x_core_groups)

    input_grad = input_grad_of(hidden, gain[None, :], cotangent, parts)
    with jax.named_scope("coefficients_over_x"):
        totals = fold(totals, input_grad)
        others = hop(totals, lambda x, y, z, c: (((x + 1) ^ 1) - 1, y, z, c))
    new_momentum = new_momentum_of(table, own_spots, own_sum, rest, own_momentum)[None]
    new_weight = new_weight_of(table, gathered, totals, others, parts, nodes)
    return (new_weight, new_momentum, input_grad)


def solution(mesh):
    return jax.shard_map(
        on_device,
        mesh=mesh,
        in_specs=(
            P(("node", "local"), None),
            P(),
            P(("node", "local"), None),
            P("local", None),
            P("node", "local", None),
            P("local", None),
        ),
        out_specs=(P(), P("node", "local", None), P(("node", "local"), None)),
        check_vma=False,
    )
```

```python
import functools

import jax
import jax.numpy as jnp
from jax import lax
from jax.experimental import pallas as pl
from jax.experimental.pallas import tpu as pltpu
from jax.sharding import PartitionSpec as P

epsilon = 1e-06
decay_rate = 0.9
learn_rate = 0.01
side = 64
pair = 128
f32 = jnp.float32
bf16 = jnp.bfloat16
kernel_room = pltpu.CompilerParams(vmem_limit_bytes=12 * 2**20)
small = pl.CostEstimate(flops=1, bytes_accessed=1, transcendentals=0)

z_groups = [[2 * z + h for z in range(8)] for h in range(2)]
core_groups = [[2 * i, 2 * i + 1] for i in range(16)]
x_core_groups = [[8 * x + 2 * r + c for x in range(4) for c in range(2)] for r in range(4)]


def whole_mesh(move):
    def index(x, y, z, core):
        return ((x * 4 + y % 4) * 2 + core) * 16 + z * 2 + y // 4

    places = [(x, y, z, c) for x in range(4) for y in range(8) for z in range(8) for c in range(2)]
    sizes = (4, 8, 8, 2)
    wrap = lambda place: [at % size for at, size in zip(place, sizes)]
    return [(index(*place), index(*wrap(move(*place)))) for place in places]


def hop(value, move):
    return lax.ppermute(value, ("node", "local"), whole_mesh(move))


def over_z(value):
    return lax.all_to_all(value, "local", 0, 0, axis_index_groups=z_groups)


def dct_table():
    freq = jnp.arange(side, dtype=f32)[:, None]
    place = jnp.arange(side, dtype=f32)[None, :]
    wave = jnp.cos(jnp.pi * (2.0 * place + 1.0) * freq / (2.0 * side))
    norm_row = jnp.where(freq == 0.0, jnp.sqrt(1.0 / side), jnp.sqrt(2.0 / side))
    return wave * norm_row


def split2(value):
    high = value.astype(bf16)
    return high, (value - high.astype(f32)).astype(bf16)


def wave_table():
    turned = dct_table().T
    high = lax.reduce_precision(turned, exponent_bits=8, mantissa_bits=7)
    low = turned - high
    empty = jnp.zeros_like(turned)
    return jnp.block([[high, empty], [low, empty], [empty, high], [empty, low]]).astype(bf16)


def dot(a, b, dims):
    return lax.dot_general(a, b, (dims, ((), ())), preferred_element_type=f32)


def from_hbm(value):
    return pltpu.with_memory_space_constraint(value, pltpu.HBM)


in_hbm = pl.BlockSpec(memory_space=pltpu.HBM)
in_vmem = pl.BlockSpec(memory_space=pltpu.VMEM)
in_smem = pl.BlockSpec(memory_space=pltpu.SMEM)


def waves(table, spots):
    tiles = spots.shape[0] // 2
    rows = jnp.concatenate([spots[at : at + 1] for at in range(tiles)], axis=1)
    cols = jnp.concatenate([spots[at : at + 1] for at in range(tiles, 2 * tiles)], axis=1)
    wide = (side, tiles * pair)
    at = lax.broadcasted_iota(jnp.int32, wide, 0)
    chosen = jnp.concatenate([jnp.where(at == rows, 1.0, 0.0), jnp.where(at == cols, 1.0, 0.0)], axis=0)
    found = dot(table, chosen.astype(bf16), ((1,), (0,)))
    block = lax.broadcasted_iota(jnp.int32, wide, 1) // 32 % 4

    def placed(value, second):
        return jnp.concatenate([jnp.where(second, 0.0, value), jnp.where(second, value, 0.0)], axis=0)

    below, right = block >= 2, block % 2 == 1
    row_high = placed(found[:side], below).astype(bf16)
    row_low = placed(found[side : 2 * side], below).astype(bf16)
    return row_high, row_low, placed(found[2 * side : 3 * side] + found[3 * side :], right)


def coded(value):
    top = jnp.max(jnp.abs(value), axis=0, keepdims=True)
    power = jnp.clip(jnp.ceil(jnp.log2(top * (1.0 / 32000.0))), -120.0, 120.0)
    whole = jnp.round(value * jnp.exp2(-power)).astype(jnp.int32)
    place = lax.broadcasted_iota(jnp.int32, (8, pair), 0)
    bits = ((power.astype(jnp.int32) + 128) >> place) & 1
    return jnp.concatenate([(whole[:8] & -2) | bits, whole[8:]], axis=0).astype(jnp.int16)


def decoded(message):
    whole = message.astype(jnp.int32)
    place = lax.broadcasted_iota(jnp.int32, (8, pair), 0)
    power = jnp.sum(((whole[:8] & 1) << place).astype(f32), axis=0, keepdims=True) - 128.0
    return whole.astype(f32) * jnp.exp2(power)


def picked_from(tile, row_high, row_low, col_waves):
    high, low = split2(tile)
    half = dot(jnp.concatenate([high, low], axis=0), jnp.concatenate([row_high, row_high], axis=0), ((0,), (0,)))
    half += dot(high, row_low, ((0,), (0,)))
    return jnp.sum(half * col_waves, axis=0, keepdims=True)


def field_from(picked, row_high, row_low, col_waves):
    high, low = split2(picked * col_waves)
    field = dot(jnp.concatenate([row_high, row_low], axis=1), jnp.concatenate([high, high], axis=1), ((1,), (1,)))
    return field + dot(row_high, low, ((1,), (1,)))


def front_kernel(
    table_ref, spots_ref, hidden_in_ref, gain_in_ref, cot_in_ref, momentum_in_ref,
    message_out_ref, high_out_ref, low_out_ref, picked_ref,
    hidden_ref, gain_ref, cot_ref, momentum_ref, message_ref, high_ref, low_ref,
    read, hidden_read, message_done, high_done, low_done,
):
    lines, _, rows, _ = message_ref.shape
    features = hidden_ref.shape[1]
    spans = [slice(line * 2 * rows, (line + 1) * 2 * rows) for line in range(lines)]
    reads = [
        pltpu.make_async_copy(source, target, read.at[at])
        for at, (source, target) in enumerate(
            [(momentum_in_ref, momentum_ref), (cot_in_ref, cot_ref), (gain_in_ref, gain_ref)]
        )
    ]
    hidden_reads = [
        pltpu.make_async_copy(hidden_in_ref.at[:, at], hidden_ref.at[:, at], hidden_read.at[line])
        for line, at in enumerate(spans)
    ]
    for copy in reads + hidden_reads:
        copy.start()
    own = waves(table_ref[...], spots_ref[...])
    reads[0].wait()
    for q in range(picked_ref.shape[0]):
        tile = decay_rate * momentum_ref[q * pair : min((q + 1) * pair, rows), :]
        short = pair - tile.shape[0]
        if short:
            tile = jnp.concatenate([tile, jnp.zeros((short, pair), f32)], axis=0)
        picked_ref[q : q + 1, :] = picked_from(tile, *[part[:, q * pair : (q + 1) * pair] for part in own])
    square = jnp.zeros((hidden_ref.shape[0], 1), f32)
    for line, at in enumerate(spans):
        hidden_reads[line].wait()
        wide = hidden_ref[:, at].astype(f32)
        square += jnp.sum(wide * wide, axis=1, keepdims=True)
    scale = lax.rsqrt(square * (1.0 / features) + epsilon)
    reads[1].wait()
    reads[2].wait()
    cot = cot_ref[...]
    copies = []
    for line, at in enumerate(spans):
        normed = (hidden_ref[:, at].astype(f32) * scale * gain_ref[:, at]).astype(bf16)
        term = dot(normed, cot, ((0,), (0,)))
        for half in range(2):
            own = term[half * rows : (half + 1) * rows]
            message_ref[line, half] = coded(own)
        high_ref[line], low_ref[line] = split2(dot(cot, normed, ((0,), (0,))))
        for source, target, done in (
            (message_ref, message_out_ref, message_done),
            (high_ref, high_out_ref, high_done),
            (low_ref, low_out_ref, low_done),
        ):
            copies.append(pltpu.make_async_copy(source.at[line], target.at[line], done.at[line]))
            copies[-1].start()
    for copy in copies:
        copy.wait()


def front(table, spots, hidden, gain, cot, momentum, owners):
    tokens, features = hidden.shape
    lines, rows = owners // 2, features // owners
    ins = (hidden, gain, cot, momentum)
    outs = (
        pltpu.HBM((lines, 2, rows, pair), jnp.int16),
        pltpu.HBM((lines, pair, 2 * rows), bf16),
        pltpu.HBM((lines, pair, 2 * rows), bf16),
    )
    return pl.pallas_call(
        front_kernel,
        out_shape=outs + (jax.ShapeDtypeStruct((spots.shape[0] // 2, pair), f32),),
        in_specs=[in_vmem, in_vmem] + [in_hbm] * 4,
        out_specs=(in_hbm,) * 3 + (in_vmem,),
        scratch_shapes=[pltpu.VMEM(value.shape, value.dtype) for value in ins + outs]
        + [pltpu.SemaphoreType.DMA((count,)) for count in (3, lines, lines, lines, lines)],
        compiler_params=kernel_room,
        cost_estimate=small,
        name="front",
    )(table, spots, *[from_hbm(value) for value in ins])


def pack_kernel(upper_ref, mine_ref, other_ref, out_ref):
    eighth = mine_ref.shape[0] - 16
    mine, other = mine_ref[...].astype(f32), other_ref[...].astype(f32)
    first = upper_ref[0] == 0
    low = jnp.where(first, mine[:eighth], other[:eighth])
    high = jnp.where(first, other[:eighth], mine[:eighth])
    packed = jnp.concatenate([low, high, mine[eighth:] + other[eighth:]], axis=0).astype(bf16)
    for target in range(out_ref.shape[0]):
        out_ref[target] = packed


def pack(upper, mine, other):
    return pl.pallas_call(
        pack_kernel,
        out_shape=jax.ShapeDtypeStruct((8, 2 * mine.shape[0] - 16, pair), bf16),
        in_specs=[in_smem, in_vmem, in_vmem],
        compiler_params=kernel_room,
        cost_estimate=small,
        name="pack",
    )(upper[None], mine, other)


def line_spots(spots_ref, line, tiles):
    tall = spots_ref.shape[1]
    spots = spots_ref[line, tall - 16 : tall, :].astype(f32).astype(jnp.int32)
    return jnp.concatenate([spots[:tiles], spots[8 : 8 + tiles]], axis=0)


def pick_kernel(
    table_ref, spots_ref, high_in_ref, low_in_ref, decayed_ref, picked_ref, high_ref, low_ref, high_done, low_done
):
    lines = spots_ref.shape[0]
    tiles = picked_ref.shape[0]
    each = tiles // lines
    arrivals = []
    for line in range(lines):
        arrivals.append(pltpu.make_async_copy(high_in_ref.at[line], high_ref.at[line], high_done.at[line]))
        arrivals.append(pltpu.make_async_copy(low_in_ref.at[line], low_ref.at[line], low_done.at[line]))
        arrivals[-2].start()
        arrivals[-1].start()
    table = table_ref[...]
    for line in range(lines):
        row_high, row_low, col_waves = waves(table, line_spots(spots_ref, line, each))
        arrivals[2 * line].wait()
        arrivals[2 * line + 1].wait()
        for tile in range(each):
            q = line * each + tile
            at = slice(tile * pair, (tile + 1) * pair)
            high = high_ref[line, :, at]
            both = jnp.concatenate([high, low_ref[line, :, at]], axis=1)
            half = dot(both, jnp.concatenate([row_high[:, at], row_high[:, at]], axis=0), ((1,), (0,)))
            half += dot(high, row_low[:, at], ((1,), (0,)))
            picked_ref[q : q + 1, :] = decayed_ref[q : q + 1, :] + jnp.sum(
                half * col_waves[:, at], axis=0, keepdims=True
            )


def pick(table, spots, high, low, decayed):
    lines = spots.shape[0]
    return pl.pallas_call(
        pick_kernel,
        out_shape=jax.ShapeDtypeStruct(decayed.shape, f32),
        in_specs=[in_vmem, in_vmem, in_hbm, in_hbm, in_vmem],
        scratch_shapes=[pltpu.VMEM(high.shape, bf16)] * 2 + [pltpu.SemaphoreType.DMA((lines,))] * 2,
        compiler_params=kernel_room,
        cost_estimate=small,
        name="pick",
    )(table, spots, from_hbm(high), from_hbm(low), decayed)


def middle_kernel(upper_ref, message_ref, total_ref, own_ref, rest_out_ref, spread_ref, rest_ref, rest_done):
    sources, halves, _, _ = message_ref.shape
    sums = []
    for half in range(halves):
        term = jnp.zeros(own_ref.shape, f32)
        for source in range(sources):
            term += decoded(message_ref[source, half])
        sums.append(term)
    first = upper_ref[0] == 0
    own_ref[...] = jnp.where(first, sums[0], sums[1])
    rest_ref[...] = coded(jnp.where(first, sums[1], sums[0]))
    copy = pltpu.make_async_copy(rest_ref, rest_out_ref, rest_done)
    copy.start()
    for source in range(sources):
        spread_ref[source] = total_ref[...]
    copy.wait()


def middle(message, upper, total):
    sources, _, rows, _ = message.shape
    return pl.pallas_call(
        middle_kernel,
        out_shape=(
            jax.ShapeDtypeStruct((rows, pair), f32),
            pltpu.HBM((rows, pair), jnp.int16),
            jax.ShapeDtypeStruct((sources,) + total.shape, f32),
        ),
        out_specs=(in_vmem, in_hbm, in_vmem),
        scratch_shapes=[pltpu.VMEM((rows, pair), jnp.int16), pltpu.SemaphoreType.DMA],
        in_specs=[in_smem, in_vmem, in_vmem],
        compiler_params=kernel_room,
        cost_estimate=small,
        name="middle",
    )(upper[None], message, total)


def momentum_kernel(table_ref, spots_ref, sum_ref, rest_ref, momentum_ref, out_ref, mid_ref):
    rows = out_ref.shape[0]
    row_high, row_low, col_waves = waves(table_ref[...], spots_ref[...])
    total = decay_rate * momentum_ref[...] + sum_ref[...]
    mid_ref[0:rows, :] = total + decoded(rest_ref[...])
    mid_ref[rows:, :] = jnp.zeros((mid_ref.shape[0] - rows, pair), f32)
    for q in range(mid_ref.shape[0] // pair):
        at = slice(q * pair, (q + 1) * pair)
        own = row_high[:, at], row_low[:, at], col_waves[:, at]
        tile = mid_ref[at, :]
        sent = field_from(picked_from(tile, *own), *own)
        left = min(pair, rows - q * pair)
        out_ref[q * pair : q * pair + left, :] = (tile - sent)[:left]


def new_momentum_of(table, spots, own_sum, rest, momentum):
    return pl.pallas_call(
        momentum_kernel,
        out_shape=jax.ShapeDtypeStruct(momentum.shape, f32),
        scratch_shapes=[pltpu.VMEM((spots.shape[0] // 2 * pair, pair), f32)],
        compiler_params=kernel_room,
        cost_estimate=small,
        name="momentum_step",
    )(table, spots, own_sum, rest, momentum)


def fold_kernel(parts_ref, _, out_ref):
    total = parts_ref[0]
    for part in range(1, parts_ref.shape[0]):
        total += parts_ref[part]
    out_ref[...] = total


def fold(parts, after):
    return pl.pallas_call(
        fold_kernel,
        out_shape=jax.ShapeDtypeStruct(parts.shape[1:], f32),
        in_specs=[in_vmem, in_hbm],
        compiler_params=kernel_room,
        cost_estimate=small,
        name="fold",
    )(parts, from_hbm(after))


def weight_rows(parts_ref, line):
    parts = [parts_ref[part, line].astype(f32) for part in range(parts_ref.shape[0])]
    eighth = parts[0].shape[0] // 2
    return jnp.concatenate([p[:eighth] for p in parts] + [p[eighth:] for p in parts], axis=0)


def weight_kernel(nodes, table_ref, spots_ref, total_ref, other_ref, parts_ref, out_ref):
    lines = spots_ref.shape[0]
    total = (total_ref[...] + other_ref[...]) / nodes
    each = total.shape[0] // lines
    table = table_ref[...]
    for line in range(lines):
        weight = weight_rows(parts_ref, line)
        row_high, row_low, col_waves = waves(table, line_spots(spots_ref, line, each))
        mean = jnp.concatenate([total[line * each + tile : line * each + tile + 1] for tile in range(each)], axis=1)
        for tile in range(each):
            q = line * each + tile
            at = slice(tile * pair, (tile + 1) * pair)
            field = field_from(mean[:, at], row_high[:, at], row_low[:, at], col_waves[:, at])
            fresh = weight[at] - learn_rate * jnp.tanh(field)
            out_ref[q * pair : (q + 1) * pair, :] = fresh.astype(bf16)


def new_weight_of(table, spots, total, other, parts, nodes):
    return pl.pallas_call(
        functools.partial(weight_kernel, nodes),
        out_shape=jax.ShapeDtypeStruct((total.shape[0] * pair, pair), bf16),
        compiler_params=kernel_room,
        cost_estimate=small,
        name="weight_step",
    )(table, spots, total, other, parts)


def input_kernel(
    hidden_ref, gain_in_ref, cot_in_ref, parts_in_ref, out_ref, gain_ref, cot_ref, parts_ref, gained_ref, read
):
    lines = parts_ref.shape[1]
    features = hidden_ref.shape[1]
    step = features // lines
    spans = [slice(line * step, (line + 1) * step) for line in range(lines)]
    reads = [
        pltpu.make_async_copy(source, target, read.at[at])
        for at, (source, target) in enumerate(
            [(parts_in_ref, parts_ref), (cot_in_ref, cot_ref), (gain_in_ref, gain_ref)]
        )
    ]
    for copy in reads:
        copy.start()
    square = jnp.zeros((hidden_ref.shape[0], 1), f32)
    for at in spans:
        wide = hidden_ref[:, at].astype(f32)
        square += jnp.sum(wide * wide, axis=1, keepdims=True)
    scale = lax.rsqrt(square * (1.0 / features) + epsilon)
    for copy in reads:
        copy.wait()
    cot = cot_ref[...]
    along = jnp.zeros(scale.shape, f32)
    for line, at in enumerate(spans):
        weight = weight_rows(parts_ref, line).astype(bf16)
        gained = gain_ref[:, at] * dot(cot, weight, ((1,), (1,)))
        gained_ref[:, at] = gained
        along += jnp.sum(hidden_ref[:, at].astype(f32) * gained, axis=1, keepdims=True)
    factor = scale**3 * (along * (1.0 / features))
    for at in spans:
        out_ref[:, at] = (scale * gained_ref[:, at] - hidden_ref[:, at].astype(f32) * factor).astype(bf16)


def input_grad_of(hidden, gain, cot, parts):
    ins = (gain, cot, parts)
    return pl.pallas_call(
        input_kernel,
        out_shape=jax.ShapeDtypeStruct(hidden.shape, bf16),
        in_specs=[in_vmem] + [in_hbm] * 3,
        scratch_shapes=[pltpu.VMEM(value.shape, value.dtype) for value in ins]
        + [pltpu.VMEM(hidden.shape, f32), pltpu.SemaphoreType.DMA((3,))],
        compiler_params=kernel_room,
        cost_estimate=small,
        name="input_gradient",
    )(hidden, *[from_hbm(value) for value in ins])


def on_device(hidden, gain, cotangent, weight, momentum, indices):
    nodes, owners = lax.axis_size("node"), lax.axis_size("local")
    node, local = lax.axis_index("node"), lax.axis_index("local")
    features = hidden.shape[1]
    own_rows, head = weight.shape
    table = wave_table()
    blocks = indices.size
    row_of, col_of = indices >> 6, indices & (side - 1)

    upper = local % 2
    eighth = own_rows // 8
    part = (node // 8) * 2 + node % 2
    with jax.named_scope("weight_part"):
        piece = lax.dynamic_slice_in_dim(weight, part * eighth, eighth, axis=0)
        at_half = lambda spots: lax.dynamic_update_slice(
            jnp.zeros((8 * pair,), jnp.int32), spots.reshape(-1), (upper * blocks,)
        ).reshape(8, pair)
        piece = jnp.concatenate([piece, at_half(row_of).astype(bf16), at_half(col_of).astype(bf16)], axis=0)
    with jax.named_scope("weight_over_y"):
        other = hop(piece, lambda x, y, z, c: (x, (y + (2 if y in (2, 3, 6, 7) else 6)) % 8, z, c))

    spare = (-blocks) % pair
    tiles = (blocks + spare) // pair
    own_spots = jnp.stack([row_of.reshape(-1), col_of.reshape(-1)])
    own_spots = jnp.pad(own_spots, ((0, 0), (0, spare))).reshape(2 * tiles, pair)
    own_momentum = momentum[0]
    with jax.named_scope("weight_over_z"):
        gathered = over_z(pack(upper, piece, other))

    message, high, low, decayed = front(table, own_spots, hidden, gain[None, :], cotangent, own_momentum, owners)
    decayed = lax.dynamic_update_slice(
        jnp.zeros((owners * blocks,), f32), decayed.reshape(-1)[:blocks], (local * blocks,)
    ).reshape(-1, pair)
    with jax.named_scope("gradient_exchange"):
        arrived = over_z(message)

    total = pick(table, gathered, high, low, decayed)
    with jax.named_scope("coefficients"):
        total = jnp.sum(lax.all_gather(total, "node", axis_index_groups=core_groups), axis=0)
        total = total + hop(total, lambda x, y, z, c: (x, y ^ 1, z, c))
        total = total + hop(total, lambda x, y, z, c: (x, ((y + 1) ^ 1) - 1, z, c))
        total = total + hop(total, lambda x, y, z, c: (x, y ^ 3 if y in (0, 3, 4, 7) else 7 - y, z, c))
        total = total + hop(total, lambda x, y, z, c: (x ^ 1, y, z, c))
    own_sum, rest, spread = middle(arrived, upper, total)
    with jax.named_scope("coefficients_over_z"):
        totals = over_z(spread)
    with jax.named_scope("gradient_over_y"):
        rest = hop(rest, lambda x, y, z, c: (x, (y + 4) % 8, z, c))

    with jax.named_scope("weight_over_x_and_core"):
        parts = lax.all_gather(gathered[:, : 2 * eighth, :], "node", axis_index_groups=x_core_groups)

    input_grad = input_grad_of(hidden, gain[None, :], cotangent, parts)
    with jax.named_scope("coefficients_over_x"):
        totals = fold(totals, input_grad)
        others = hop(totals, lambda x, y, z, c: (((x + 1) ^ 1) - 1, y, z, c))
    new_momentum = new_momentum_of(table, own_spots, own_sum, rest, own_momentum)[None]
    new_weight = new_weight_of(table, gathered, totals, others, parts, nodes)
    return (new_weight, new_momentum, input_grad)


def solution(mesh):
    return jax.shard_map(
        on_device,
        mesh=mesh,
        in_specs=(
            P(("node", "local"), None),
            P(),
            P(("node", "local"), None),
            P("local", None),
            P("node", "local", None),
            P("local", None),
        ),
        out_specs=(P(), P("node", "local", None), P(("node", "local"), None)),
        check_vma=False,
    )
```
